256 devices in a mesh: expert: 4 (over y), tensor: 16 (over x, z_lo, core), dp: 4 (over z_hi).
Axes of the slice: x: 4, y: 4, z: 8 (z_hi: 4, z_lo: 2; z = z_hi * 2 + z_lo), core: 2. Of those that a mesh axis runs over, the one named last changes fastest.
Arguments:
- tokens: bfloat16 [32768, 3072], P(('dp', 'expert', 'tensor')), parts along dimension 0, may hold values from -6 to 6
- routes: int32 [32768, 2], P(('dp', 'expert', 'tensor')), parts along dimension 0, may hold values from 0 to 7, as said below
- language: int32 [32768], P(('dp', 'expert', 'tensor')), parts along dimension 0, may hold values from 0 to 100
- teacher: bfloat16 [32768, 3072], P(('dp', 'expert', 'tensor')), parts along dimension 0, may hold values from -33 to 33
- router_weight: bfloat16 [3072, 8], replicated, may hold values from -0.109375 to 0.109375
- gate_weight: bfloat16 [3072, 8192], P(None, 'tensor'), may hold values from -0.109375 to 0.109375
- up_weight: bfloat16 [3072, 8192], P(None, 'tensor'), may hold values from -0.109375 to 0.109375
- down_weight: bfloat16 [8192, 3072], P('tensor'), may hold values from -0.0625 to 0.0625
Outputs:
- layer_out: bfloat16 [32768, 3072], P(('dp', 'expert', 'tensor')), parts along dimension 0
- grad_tokens: bfloat16 [32768, 3072], P(('dp', 'expert', 'tensor')), parts along dimension 0
- grad_router: float32 [12288, 8], P('dp'), parts along dimension 0
- lang_loss: float32 [404], P('dp'), parts along dimension 0
The draws below stay inside these ranges and needn't reach their ends.
There are 4 independent parts, one for each index of `dp`. The reference program is written for one: setup_inputs(seed, part) draws one part's arguments, and reference() takes and returns one part's arrays. A program takes and returns all parts, laid end to end along the dimension named above; an argument that names none is the same for every part. Nothing has to cross between parts.
Inputs may be any that keep to these rules, and one draw needn't show every extreme that they name: `routes`: each row names two different experts. Among the rows of one device (aligned blocks of 128 rows) at most 32 name expert 0; in every draw each block of some run of 2048 rows starting at a multiple of it has exactly 32 such rows.
All inputs are finite; a program needn't handle non-finite values.
Results may differ from the reference program's by a relative error of at most 0.015.
Values may be sent and summed in bfloat16 or wider, within the bound.
No kernel may reach another device: no remote copies, remote signals or barrier semaphores. Data moves between devices by JAX's collectives and lax.ppermute only.
A program may use at most 128 MiB of HBM per device.

```python
import math
from functools import partial
import jax
import jax.numpy as jnp
import numpy as np
from jax import lax

D = 3072
FF = 8192
EXPERTS = 8
LANGS = 101
TOK_DEV = 128
CAP = 32
TOKENS = 8192
N_EXPERT = 4
N_TENSOR = 16


def draw_routes(key, part):
    blocks = TOKENS // TOK_DEV
    group_blocks = blocks // N_EXPERT
    key_load, key_group, key_order, key_first, key_offset, key_swap = jax.random.split(key, 6)
    slot_loads = jax.random.randint(key_load, (blocks,), 1, CAP + 1)
    full_group = jax.random.randint(key_group, (), 0, N_EXPERT)
    block_ids = jnp.arange(blocks, dtype=jnp.int32)
    slot_loads = jnp.where(block_ids // group_blocks == full_group, CAP, slot_loads)
    scores = jax.random.randint(key_order, (blocks, TOK_DEV), 0, 1 << 20) * TOK_DEV
    scores = scores + lax.broadcasted_iota(jnp.int32, (blocks, TOK_DEV), 1)
    ordering = jnp.argsort(scores, axis=1)
    position = jnp.argsort(ordering, axis=1)
    chosen = position < slot_loads[:, None]
    first_pick = jax.random.randint(key_first, (blocks, TOK_DEV), 1, EXPERTS)
    offset = jax.random.randint(key_offset, (blocks, TOK_DEV), 1, EXPERTS - 1)
    second_pick = 1 + (first_pick - 1 + offset) % (EXPERTS - 1)
    partner = jnp.where(chosen, 0, second_pick)
    swapped = jax.random.randint(key_swap, (blocks, TOK_DEV), 0, 2)
    column_one = jnp.where(swapped == 1, partner, first_pick)
    column_two = jnp.where(swapped == 1, first_pick, partner)
    return jnp.stack([column_one, column_two], -1).reshape(TOKENS, 2).astype(jnp.int32)


def draw_teacher(key, part):
    key_base, key_row, key_col = jax.random.split(key, 3)
    row_pos = lax.broadcasted_iota(jnp.float32, (TOKENS, 1), 0) / (TOKENS - 1)
    row_jitter = jax.random.uniform(key_row, (TOKENS, 1), jnp.float32)
    col_jitter = jax.random.uniform(key_col, (1, D), jnp.float32)
    row_scale = jnp.exp(math.log(3.2) * (row_pos + row_jitter))
    col_scale = jnp.exp(math.log(3.2) * col_jitter)
    base = jnp.clip(jax.random.normal(key_base, (TOKENS, D), jnp.float32), -4.0, 4.0)
    return (0.25 * base * row_scale * col_scale).astype(jnp.bfloat16)


def place_ends(values, stream_key, low, high):
    spot = [jax.random.randint(jax.random.fold_in(stream_key, axis), (), 0, length) for axis, length in enumerate(values.shape)]
    widest = values.shape.index(max(values.shape))
    beside = spot[:widest] + [(spot[widest] + 1) % values.shape[widest]] + spot[widest + 1:]
    return values.at[tuple(spot)].set(low).at[tuple(beside)].set(high)


def level_of(key, shape, cuts, smallest, largest):
    factor_of, own = 1.0, jax.random.fold_in(key, 6)
    for axis_at, blocks in cuts:
        draws = jnp.exp(jax.random.uniform(jax.random.fold_in(own, axis_at), (blocks,), jnp.float32, smallest / len(cuts), largest / len(cuts)))
        factor_of = factor_of * jnp.repeat(draws, shape[axis_at] // blocks).reshape([-1 if axis == axis_at else 1 for axis in range(len(shape))])
    return factor_of


def cumulative_ranks(amount, slope):
    portions = [(1 << 20) // math.isqrt(grade ** slope) + 1 for grade in range(1, amount + 1)]
    spread = 1 + sum(portions) // (1 << 30)
    return np.cumsum(np.array([max(1, weight // spread) for weight in portions]))


def skewed_ids(rng, shape, count, slope):
    grid = cumulative_ranks(count, slope)
    pick = jax.random.randint(jax.random.fold_in(rng, 1), shape, 0, int(grid[count - 1]))
    rank = jnp.searchsorted(jnp.asarray(grid, jnp.int32), pick, side="right")
    return jax.random.permutation(jax.random.fold_in(rng, 2), count)[rank].astype(jnp.int32)


def gaussian(rng, extent, scale, bound, pieces=(), kind=jnp.bfloat16):
    array = jax.random.normal(rng, extent, jnp.float32) * scale
    if len(pieces) > 0:
        array = level_of(rng, extent, pieces, -0.22, 0.18) * array
    return jnp.clip(array, min=-bound, max=bound).astype(kind)


def setup_inputs(seed: int = 0, part: int = 0) -> dict:
    seeds = jax.random.split(jax.random.key(seed), 9)
    part_keys = jax.random.split(jax.random.fold_in(seeds[8], part), 9)
    return {
        "tokens": gaussian(part_keys[0], (TOKENS, D), 1.0, 6.0, ((0, 64),)),
        "routes": draw_routes(jax.random.fold_in(jax.random.fold_in(seeds[8], part), 71), part),
        "language": place_ends(skewed_ids(part_keys[2], (TOKENS,), LANGS, 3), jax.random.fold_in(part_keys[2], 3), 0, LANGS - 1).astype(jnp.int32),
        "teacher": draw_teacher(jax.random.fold_in(jax.random.fold_in(seeds[8], part), 71), part),
        "router_weight": gaussian(seeds[4], (D, EXPERTS), D ** -0.5, 0.109375),
        "gate_weight": gaussian(seeds[5], (D, FF), D ** -0.5, 0.109375, ((1, 16),)),
        "up_weight": gaussian(seeds[6], (D, FF), D ** -0.5, 0.109375, ((1, 16),)),
        "down_weight": gaussian(seeds[7], (FF, D), FF ** -0.5, 0.0625, ((0, 16),)),
    }


highest = lax.Precision.HIGHEST
CONTRACT_LAST = (((1,), (1,)), ((), ()))


def routing(tokens, routes, router_weight):
    logits = jnp.dot(tokens, router_weight, preferred_element_type=jnp.float32)
    first_id = routes[:, 0]
    second_id = routes[:, 1]
    chosen = jnp.logical_or(first_id == 0, second_id == 0)
    other_id = jnp.where(first_id == 0, second_id, first_id)
    columns = lax.broadcasted_iota(jnp.int32, logits.shape, 1)
    other_hot = (columns == other_id[:, None]).astype(jnp.float32)
    own_hot = (columns == 0).astype(jnp.float32)
    margin = logits[:, 0] - jnp.sum(logits * other_hot, axis=1)
    squash = jax.nn.sigmoid(margin)
    chosen_mask = chosen.astype(jnp.float32)
    return chosen, chosen_mask * squash, chosen_mask * squash * (1.0 - squash), own_hot - other_hot


def placing_matrix(chosen, capacity):
    slot_rank = jnp.cumsum(chosen.astype(jnp.int32)) - 1
    slot_ids = lax.broadcasted_iota(jnp.int32, (chosen.shape[0], capacity), 1)
    return jnp.logical_and(slot_rank[:, None] == slot_ids, chosen[:, None]).astype(jnp.float32)


def reference(tokens, routes, language, teacher, router_weight, gate_weight, up_weight, down_weight):
    blocks = TOKENS // TOK_DEV
    block_width = FF // N_TENSOR
    slot_rows = blocks * CAP
    chosen, gate_value, gate_slope, direction = routing(tokens, routes, router_weight)
    placing = jax.vmap(partial(placing_matrix, capacity=CAP))(chosen.reshape(blocks, TOK_DEV))
    token_blocks = tokens.astype(jnp.float32).reshape(blocks, TOK_DEV, D)
    token_slots = jnp.einsum("btc,btd->bcd", placing, token_blocks, precision=highest)
    token_slots = token_slots.astype(jnp.bfloat16).reshape(slot_rows, D)
    pre_gate = jnp.dot(token_slots, gate_weight, preferred_element_type=jnp.float32)
    pre_up = jnp.dot(token_slots, up_weight, preferred_element_type=jnp.float32)
    hidden = (jax.nn.silu(pre_gate) * pre_up).astype(jnp.bfloat16)

    def down_block(block_index, running):
        start_col = (block_index * block_width).astype(jnp.int32)
        part_hidden = lax.dynamic_slice_in_dim(hidden, start_col, block_width, 1)
        part_down = lax.dynamic_slice_in_dim(down_weight, start_col, block_width, 0)
        rounded = jnp.dot(part_hidden, part_down, preferred_element_type=jnp.float32).astype(jnp.bfloat16)
        rounded = lax.optimization_barrier(rounded)
        return running + rounded.astype(jnp.float32)

    expert_slots = lax.fori_loop(0, N_TENSOR, down_block, jnp.zeros((slot_rows, D), jnp.float32))
    expert_rows = jnp.einsum("btc,bcd->btd", placing, expert_slots.reshape(blocks, CAP, D), precision=highest).reshape(TOKENS, D)
    combined = tokens.astype(jnp.float32) + gate_value[:, None] * expert_rows
    layer_out = combined.astype(jnp.bfloat16)
    deviation = combined - teacher.astype(jnp.float32)
    loss_tok = 0.5 * jnp.mean(deviation * deviation, axis=1)
    lang_hot = (language[:, None] == lax.broadcasted_iota(jnp.int32, (TOKENS, LANGS), 1)).astype(jnp.float32)
    lang_sums = jnp.dot(loss_tok, lang_hot, precision=highest)
    lang_counts = jnp.sum(lang_hot, axis=0)
    lang_loss = lang_sums / jnp.maximum(lang_counts, 1.0)

    gate_dot = jnp.sum(deviation * expert_rows, axis=1)
    dlogits = (gate_dot * gate_slope)[:, None] * direction
    grad_router = jnp.dot(tokens.astype(jnp.float32).T, dlogits, precision=highest) / TOKENS
    expert_grad = (gate_value[:, None] * deviation).astype(jnp.bfloat16)
    grad_blocks = expert_grad.astype(jnp.float32).reshape(blocks, TOK_DEV, D)
    grad_slots = jnp.einsum("btc,btd->bcd", placing, grad_blocks, precision=highest)
    grad_slots = grad_slots.astype(jnp.bfloat16).reshape(slot_rows, D)
    back_hidden = lax.dot_general(grad_slots, down_weight, CONTRACT_LAST, preferred_element_type=jnp.float32)
    squash = jax.nn.sigmoid(pre_gate)
    grad_pre_gate = (back_hidden * pre_up * squash * (1.0 + pre_gate * (1.0 - squash))).astype(jnp.bfloat16)
    grad_pre_up = (back_hidden * pre_gate * squash).astype(jnp.bfloat16)

    def back_block(block_index, running):
        start_col = (block_index * block_width).astype(jnp.int32)
        part_gate = lax.dynamic_slice_in_dim(grad_pre_gate, start_col, block_width, 1)
        part_up = lax.dynamic_slice_in_dim(grad_pre_up, start_col, block_width, 1)
        weight_gate = lax.dynamic_slice_in_dim(gate_weight, start_col, block_width, 1)
        weight_up = lax.dynamic_slice_in_dim(up_weight, start_col, block_width, 1)
        summed = lax.dot_general(part_gate, weight_gate, CONTRACT_LAST, preferred_element_type=jnp.float32)
        summed = summed + lax.dot_general(part_up, weight_up, CONTRACT_LAST, preferred_element_type=jnp.float32)
        rounded = lax.optimization_barrier(summed.astype(jnp.bfloat16))
        return running + rounded.astype(jnp.float32)

    back_slots = lax.fori_loop(0, N_TENSOR, back_block, jnp.zeros((slot_rows, D), jnp.float32))
    back_rows = jnp.einsum("btc,bcd->btd", placing, back_slots.reshape(blocks, CAP, D), precision=highest).reshape(TOKENS, D)
    router_back = jnp.dot(dlogits, router_weight.astype(jnp.float32).T, precision=highest)
    grad_tokens = (deviation + back_rows + router_back).astype(jnp.bfloat16)
    return layer_out, grad_tokens, grad_router, lang_loss
```

```python
import functools

import jax
import jax.numpy as jnp
from jax import lax
from jax.experimental import pallas as pl
from jax.experimental.pallas import tpu as pltpu
from jax.sharding import Mesh
from jax.sharding import PartitionSpec as P

LANGS = 101
LANES = 128
TILE = 256
BLOCKS = 8
NT = (((1,), (1,)), ((), ()))
TN = (((0,), (0,)), ((), ()))
f32 = jnp.float32
bf16 = jnp.bfloat16
GROUP = ("x", "z", "core")


def move(value, target):
    pairs = []
    for x in range(4):
        for z in range(2):
            for c in range(2):
                tx, tz, tc = target(x, z, c)
                pairs.append(((x * 2 + z) * 2 + c, ((tx % 4) * 2 + tz % 2) * 2 + tc % 2))
    return lax.ppermute(value, GROUP, pairs)


def ahead(value):
    return move(value, lambda x, z, c: (x + 1 - 2 * c, z, c))


def behind(value):
    return move(value, lambda x, z, c: (x - 1 + 2 * c, z, c))


def across(value):
    return move(value, lambda x, z, c: (x, z + 1, c))


def twin(value):
    return move(value, lambda x, z, c: (x, z, c + 1))


def gather(own):
    z0 = across(own)
    f1 = ahead(own)
    b1 = behind(own)
    zb1 = behind(z0)
    x2 = ahead(f1)
    zf1 = across(f1)
    zx2 = behind(zb1)
    return [own, f1, b1, x2, z0, zf1, zb1, zx2]


def add(*parts):
    return sum(p.astype(f32) for p in parts).astype(bf16)


def scatter_sum(terms):
    own, f1, b1, x2, z0, zf1, zb1, zx2 = terms
    got_zb1 = ahead(zx2)
    got_x2 = behind(x2)
    got_zf1 = across(zf1)
    got_b1 = ahead(b1)
    got_z0 = ahead(add(zb1, got_zb1))
    got_f1 = behind(add(f1, got_x2, got_zf1))
    got_z = across(add(z0, got_z0))
    return own.astype(f32) + got_b1.astype(f32) + got_f1.astype(f32) + got_z.astype(f32)


def forward_kernel(*refs):
    blocks = refs[:BLOCKS]
    weights = refs[BLOCKS : BLOCKS + 6]
    outs = refs[BLOCKS + 6 : 2 * BLOCKS + 6]
    pre_gate, pre_up = refs[2 * BLOCKS + 6 : 2 * BLOCKS + 8]
    rows, gate_buf, up_buf, down_buf, hidden, row_sem, gate_sem, up_sem, down_sem = refs[2 * BLOCKS + 8 :]
    gates, ups, downs = weights[0:2], weights[2:4], weights[4:6]
    each = blocks[0].shape[0]
    width = gates[0].shape[1]
    per = width // TILE
    tiles = 2 * per
    copies = []
    for b in range(BLOCKS):
        copies.append(pltpu.make_async_copy(blocks[b], rows.at[pl.ds(b * each, each)], row_sem.at[b]))
    gate_copies, up_copies, down_copies = [], [], []
    for t in range(tiles):
        half, col = t // per, (t % per) * TILE
        gate_copies.append(pltpu.make_async_copy(gates[half].at[:, pl.ds(col, TILE)], gate_buf.at[t], gate_sem.at[t]))
        up_copies.append(pltpu.make_async_copy(ups[half].at[:, pl.ds(col, TILE)], up_buf.at[t], up_sem.at[t]))
        down_copies.append(pltpu.make_async_copy(downs[half].at[pl.ds(col, TILE)], down_buf.at[pl.ds(t * TILE, TILE)], down_sem.at[t]))
    for c in copies:
        c.start()
    for t in range(tiles):
        gate_copies[t].start()
        up_copies[t].start()
    for t in range(tiles):
        down_copies[t].start()
    for c in copies:
        c.wait()
    for t in range(tiles):
        gate_copies[t].wait()
        gate = jnp.dot(rows[...], gate_buf[t], preferred_element_type=f32)
        up_copies[t].wait()
        up = jnp.dot(rows[...], up_buf[t], preferred_element_type=f32)
        pre_gate[:, t * TILE : (t + 1) * TILE] = gate
        pre_up[:, t * TILE : (t + 1) * TILE] = up
        hidden[:, t * TILE : (t + 1) * TILE] = (gate * jax.nn.sigmoid(gate) * up).astype(bf16)
    for c in down_copies:
        c.wait()

    @pl.loop(0, rows.shape[1] // TILE)
    def _(n):
        cols = pl.ds(pl.multiple_of(n * TILE, TILE), TILE)
        part = jnp.dot(hidden[...], down_buf[:, cols], preferred_element_type=f32).astype(bf16)
        for b in range(BLOCKS):
            outs[b][:, cols] = part[b * each : (b + 1) * each]


def forward(blocks, gates, ups, downs):
    each, width = blocks[0].shape
    hid = 2 * gates[0].shape[1]
    tiles = hid // TILE
    rows = BLOCKS * each
    anyspec = pl.BlockSpec(memory_space=pl.ANY)
    vmem = pl.BlockSpec(memory_space=pltpu.VMEM)
    res = pl.pallas_call(
        forward_kernel,
        name="expert_forward",
        out_shape=[jax.ShapeDtypeStruct((each, width), bf16)] * BLOCKS + [jax.ShapeDtypeStruct((rows, hid), f32)] * 2,
        in_specs=[anyspec] * (BLOCKS + 6),
        out_specs=[vmem] * (BLOCKS + 2),
        scratch_shapes=[
            pltpu.VMEM((rows, width), bf16),
            pltpu.VMEM((tiles, width, TILE), bf16),
            pltpu.VMEM((tiles, width, TILE), bf16),
            pltpu.VMEM((hid, width), bf16),
            pltpu.VMEM((rows, hid), bf16),
            pltpu.SemaphoreType.DMA((BLOCKS,)),
            pltpu.SemaphoreType.DMA((tiles,)),
            pltpu.SemaphoreType.DMA((tiles,)),
            pltpu.SemaphoreType.DMA((tiles,)),
        ],
        compiler_params=pltpu.CompilerParams(vmem_limit_bytes=40 << 20),
        cost_estimate=pl.CostEstimate(flops=6 * rows * width * hid, bytes_accessed=6 * width * hid, transcendentals=rows * hid),
    )(*blocks, *gates, *ups, *downs)
    return list(res[:BLOCKS]), res[BLOCKS], res[BLOCKS + 1]


def backward_kernel(*refs):
    blocks = refs[:BLOCKS]
    weights = refs[BLOCKS : BLOCKS + 6]
    pre_gate, pre_up = refs[BLOCKS + 6 : BLOCKS + 8]
    outs = refs[BLOCKS + 8 : 2 * BLOCKS + 8]
    rows, gate_buf, up_buf, down_buf, gate_grad, up_grad, row_sem, weight_sem, down_sem = refs[2 * BLOCKS + 8 :]
    gates, ups, downs = weights[0:2], weights[2:4], weights[4:6]
    each = blocks[0].shape[0]
    width = gates[0].shape[1]
    per = width // TILE
    tiles = 2 * per
    copies = []
    for b in range(BLOCKS):
        copies.append(pltpu.make_async_copy(blocks[b], rows.at[pl.ds(b * each, each)], row_sem.at[b]))
    down_copies = []
    for t in range(tiles):
        half, row = t // per, (t % per) * TILE
        down_copies.append(pltpu.make_async_copy(downs[half].at[pl.ds(row, TILE)], down_buf.at[t], down_sem.at[t]))
    weight_copies = []
    for half in range(2):
        weight_copies.append(pltpu.make_async_copy(gates[half], gate_buf.at[half], weight_sem.at[2 * half]))
        weight_copies.append(pltpu.make_async_copy(ups[half], up_buf.at[half], weight_sem.at[2 * half + 1]))
    for c in copies + down_copies + weight_copies:
        c.start()
    for c in copies:
        c.wait()
    for t in range(tiles):
        down_copies[t].wait()
        back = lax.dot_general(rows[...], down_buf[t], NT, preferred_element_type=f32)
        gate = pre_gate[:, t * TILE : (t + 1) * TILE]
        up = pre_up[:, t * TILE : (t + 1) * TILE]
        squash = jax.nn.sigmoid(gate)
        gate_grad[:, t * TILE : (t + 1) * TILE] = (back * up * squash * (1.0 + gate * (1.0 - squash))).astype(bf16)
        up_grad[:, t * TILE : (t + 1) * TILE] = (back * gate * squash).astype(bf16)
    for c in weight_copies:
        c.wait()

    @pl.loop(0, rows.shape[1] // TILE)
    def _(n):
        cols = pl.ds(pl.multiple_of(n * TILE, TILE), TILE)
        total = None
        for half in range(2):
            for grad, buf in ((gate_grad, gate_buf), (up_grad, up_buf)):
                term = lax.dot_general(grad[:, half * width : (half + 1) * width], buf[half, cols, :], NT, preferred_element_type=f32)
                total = term if total is None else total + term
        part = total.astype(bf16)
        for b in range(BLOCKS):
            outs[b][:, cols] = part[b * each : (b + 1) * each]


def backward(blocks, gates, ups, downs, pre_gate, pre_up):
    each, width = blocks[0].shape
    half = gates[0].shape[1]
    hid = 2 * half
    tiles = hid // TILE
    rows = BLOCKS * each
    anyspec = pl.BlockSpec(memory_space=pl.ANY)
    vmem = pl.BlockSpec(memory_space=pltpu.VMEM)
    return pl.pallas_call(
        backward_kernel,
        name="expert_backward",
        out_shape=[jax.ShapeDtypeStruct((each, width), bf16)] * BLOCKS,
        in_specs=[anyspec] * (BLOCKS + 6) + [vmem] * 2,
        out_specs=[vmem] * BLOCKS,
        scratch_shapes=[
            pltpu.VMEM((rows, width), bf16),
            pltpu.VMEM((2, width, half), bf16),
            pltpu.VMEM((2, width, half), bf16),
            pltpu.VMEM((tiles, TILE, width), bf16),
            pltpu.VMEM((rows, hid), bf16),
            pltpu.VMEM((rows, hid), bf16),
            pltpu.SemaphoreType.DMA((BLOCKS,)),
            pltpu.SemaphoreType.DMA((4,)),
            pltpu.SemaphoreType.DMA((tiles,)),
        ],
        compiler_params=pltpu.CompilerParams(vmem_limit_bytes=40 << 20),
        cost_estimate=pl.CostEstimate(flops=6 * rows * width * hid, bytes_accessed=6 * width * hid, transcendentals=rows * hid),
    )(*blocks, *gates, *ups, *downs, pre_gate, pre_up)


def router_kernel(*refs):
    blocks = refs[:BLOCKS]
    slopes, out = refs[BLOCKS], refs[BLOCKS + 1]
    each = blocks[0].shape[0]
    experts = out.shape[0]
    total = None
    for b in range(BLOCKS):
        term = jnp.dot(slopes[:, b * each : (b + 1) * each], blocks[b][...], preferred_element_type=f32)
        total = term if total is None else total + term
    out[...] = total[:experts] + total[experts : 2 * experts] + total[2 * experts :]


def router_sum(blocks, slopes):
    vmem = pl.BlockSpec(memory_space=pltpu.VMEM)
    return pl.pallas_call(
        router_kernel,
        name="router_sum",
        out_shape=jax.ShapeDtypeStruct((slopes.shape[0] // 3, blocks[0].shape[1]), f32),
        in_specs=[vmem] * (BLOCKS + 1),
        out_specs=vmem,
        compiler_params=pltpu.CompilerParams(vmem_limit_bytes=16 << 20),
        cost_estimate=pl.CostEstimate(flops=2 * slopes.shape[0] * 256 * 3072, bytes_accessed=2 * 256 * 3072, transcendentals=0),
    )(*blocks, slopes)


def local(tokens, routes, language, teacher, router_weight, gate_weight, up_weight, down_weight):
    tok_rows, width = tokens.shape
    capacity = tok_rows // 4
    experts = router_weight.shape[1]
    all_tokens = tok_rows * 64
    first_id = routes[:, 0]
    second_id = routes[:, 1]
    chosen = jnp.logical_or(first_id == 0, second_id == 0)
    other_id = jnp.where(first_id == 0, second_id, first_id).astype(f32)
    upper = (lax.broadcasted_iota(jnp.int32, (tok_rows, tok_rows), 0) <= lax.broadcasted_iota(jnp.int32, (tok_rows, tok_rows), 1)).astype(f32)
    rank = jnp.sum(upper * chosen.astype(f32)[:, None], axis=0) - 1.0
    slot_ids = lax.broadcasted_iota(jnp.int32, (capacity, tok_rows), 0).astype(f32)
    placing = jnp.logical_and(rank[None, :] == slot_ids, chosen[None, :]).astype(f32)
    placing_half = placing.astype(bf16)
    token_slots = jnp.dot(placing_half, tokens, preferred_element_type=f32).astype(bf16)

    token_blocks = gather(token_slots)
    gates = [gate_weight, twin(gate_weight)]
    ups = [up_weight, twin(up_weight)]
    downs = [down_weight, twin(down_weight)]

    teacher_slots = jnp.dot(placing_half, teacher, preferred_element_type=f32)
    logits = jnp.dot(token_slots, router_weight, preferred_element_type=f32)
    other_slots = jnp.sum(placing * other_id[None, :], axis=1)
    filled = jnp.sum(placing, axis=1)
    columns = lax.broadcasted_iota(jnp.int32, logits.shape, 1).astype(f32)
    other_hot = (columns == other_slots[:, None]).astype(f32)
    squash = jax.nn.sigmoid(logits[:, 0] - jnp.sum(logits * other_hot, axis=1))
    gate_value = filled * squash
    gate_slope = filled * squash * (1.0 - squash)
    plain = tokens.astype(f32) - teacher.astype(f32)
    plain_grad = plain.astype(bf16)
    plain_loss = jnp.where(chosen, 0.0, 0.5 * jnp.mean(plain * plain, axis=1))
    lang_hot = (language[:, None] == lax.broadcasted_iota(jnp.int32, (tok_rows, LANES), 1)).astype(f32)
    lang_counts = jnp.sum(lang_hot, axis=0)

    terms, pre_gate, pre_up = forward(token_blocks, gates, ups, downs)
    own_out = scatter_sum(terms)
    combined = token_slots.astype(f32) + gate_value[:, None] * own_out
    deviation = combined - teacher_slots
    grad_slots = (gate_value[:, None] * deviation).astype(bf16)
    grad_blocks = gather(grad_slots)

    slot_loss = 0.5 * jnp.mean(deviation * deviation, axis=1)
    slot_dot = jnp.sum(deviation * own_out, axis=1) * gate_slope
    row_loss = plain_loss + jnp.sum(placing * slot_loss[:, None], axis=0)
    lang_sums = jnp.sum(row_loss[:, None] * lang_hot, axis=0)
    pack = jnp.zeros((8, LANES), f32)
    pack = pack.at[0].set(lang_sums).at[1].set(lang_counts).at[2, :capacity].set(slot_dot).at[2, capacity : 2 * capacity].set(other_slots)
    both = jnp.concatenate([pack, across(pack)], 0)
    both_f = ahead(both)
    both_b = behind(both)
    both_x = ahead(both_f)
    packs = jnp.stack([both, both_f, both_b, both_x], 0).reshape(4, 2, 8, LANES).transpose(1, 0, 2, 3).reshape(BLOCKS, 8, LANES)
    lang_pack = jnp.sum(packs[:, :2], axis=0)
    all_dots = packs[:, 2, :capacity].reshape(1, BLOCKS * capacity)
    all_other = packs[:, 2, capacity : 2 * capacity].reshape(1, BLOCKS * capacity)
    row_ids = lax.broadcasted_iota(jnp.int32, (experts, BLOCKS * capacity), 0).astype(f32)
    slopes = all_dots * ((row_ids == 0).astype(f32) - (row_ids == all_other).astype(f32))
    high = slopes.astype(bf16)
    rest = slopes - high.astype(f32)
    mid = rest.astype(bf16)
    low = (rest - mid.astype(f32)).astype(bf16)
    router_part = router_sum(token_blocks, jnp.concatenate([high, mid, low], 0))
    summed = jnp.concatenate([router_part, jnp.concatenate([lang_pack, jnp.zeros((experts - 2, LANES), f32)], 0)], 1)
    summed = summed + twin(summed)
    summed = summed + sum(lax.ppermute(summed, "expert", [(i, (i + s) % 4) for i in range(4)]) for s in (1, 2, 3))
    grad_router = summed[:, :width].T / all_tokens
    lang_loss = summed[0, width : width + LANGS] / jnp.maximum(summed[1, width : width + LANGS], 1.0)

    placed = lax.dot_general(placing_half, combined.astype(bf16), TN, preferred_element_type=f32)
    layer_out = jnp.where(chosen[:, None], placed.astype(bf16), tokens)

    own_hot = (columns == 0).astype(f32)
    dlogits = slot_dot[:, None] * (own_hot - other_hot)
    router_back = lax.dot_general(dlogits, router_weight.astype(f32), NT, precision=lax.Precision.HIGHEST)
    so_far = deviation + router_back

    own_back = scatter_sum(backward(grad_blocks, gates, ups, downs, pre_gate, pre_up))
    slot_grad = (so_far + own_back).astype(bf16)
    placed_grad = lax.dot_general(placing_half, slot_grad, TN, preferred_element_type=f32)
    grad_tokens = jnp.where(chosen[:, None], placed_grad.astype(bf16), plain_grad)
    return (layer_out, grad_tokens, grad_router, lang_loss)


def solution(mesh):
    wide = Mesh(mesh.devices.reshape(4, 4, 2, 2, 4), ("expert", "x", "z", "core", "dp"))
    rows = ("dp", "expert", "x", "z", "core")
    hidden = ("x", "z", "core")
    return jax.shard_map(
        local,
        mesh=wide,
        in_specs=(
            P(rows, None),
            P(rows, None),
            P(rows),
            P(rows, None),
            P(),
            P(None, hidden),
            P(None, hidden),
            P(hidden, None),
        ),
        out_specs=(P(rows, None), P(rows, None), P("dp", None), P("dp")),
        check_vma=False,
    )
```

```python
import functools

import jax
import jax.numpy as jnp
from jax import lax
from jax.experimental import pallas as pl
from jax.experimental.pallas import tpu as pltpu
from jax.sharding import Mesh
from jax.sharding import PartitionSpec as P

LANGS = 101
LANES = 128
TILE = 256
BLOCKS = 8
PLANE = 4
NT = (((1,), (1,)), ((), ()))
TN = (((0,), (0,)), ((), ()))
f32 = jnp.float32
bf16 = jnp.bfloat16
GROUP = ("x", "z", "core", "dp")


def move(value, target):
    pairs = []
    for x in range(4):
        for z in range(8):
            for c in range(2):
                tx, tz, tc = target(x, z, c)
                spots = [((px % 4 * 2 + pz % 2) * 2 + pc) * 4 + pz % 8 // 2 for px, pz, pc in ((x, z, c), (tx, tz, tc))]
                pairs.append(tuple(spots))
    return lax.ppermute(value, GROUP, pairs)


def facing(z, c):
    return z + 1 - 2 * ((z + c) % 2)


def ahead(value):
    return move(value, lambda x, z, c: (x + 1 - 2 * c, z, c))


def behind(value):
    return move(value, lambda x, z, c: (x - 1 + 2 * c, z, c))


def across(value):
    return move(value, lambda x, z, c: (x, facing(z, c), c))


def ahead_across(value):
    return move(value, lambda x, z, c: (x + 1 - 2 * c, facing(z, c), c))


def behind_across(value):
    return move(value, lambda x, z, c: (x - 1 + 2 * c, facing(z, c), c))


def twin(value):
    return move(value, lambda x, z, c: (x, z, 1 - c))


def pair(value):
    return move(value, lambda x, z, c: (x, z + 1 - 2 * (z % 2), c))


def after(value, *others):
    return lax.optimization_barrier((value, *others))[0]


def gather(own):
    f1 = ahead(own)
    zb1 = behind_across(own)
    b1 = behind(own)
    z0 = across(own)
    zf1 = ahead_across(own)
    x2 = ahead(f1)
    zx2 = behind(zb1)
    return [own, f1, b1, x2, z0, zf1, zb1, zx2]


def add(*parts):
    return sum(p.astype(f32) for p in parts).astype(bf16)


def scatter(terms):
    own, f1, b1, x2, z0, zf1, zb1, zx2 = terms
    got_zx2 = ahead_across(zx2)
    got_x2 = behind(x2)
    got_zf1 = across(zf1)
    got_zb1 = across(zb1)
    got_z0 = across(z0)
    got_f1 = behind(add(f1, got_x2, got_zf1))
    got_b1 = ahead(add(b1, got_zb1, got_zx2))
    return [own, got_z0, got_f1, got_b1]


def stack_rows(blocks, rows):
    each, width = blocks[0].shape[0], rows.shape[1]
    for b, block in enumerate(blocks):
        rows[b * each : (b + 1) * each] = block[:, :width]


VMEM = pl.BlockSpec(memory_space=pltpu.VMEM)


def hidden_kernel(*refs):
    blocks, gates, ups = refs[:BLOCKS], refs[BLOCKS : BLOCKS + 2], refs[BLOCKS + 2 : BLOCKS + 4]
    hidden, pre_gate, pre_up, rows = refs[BLOCKS + 4 :]
    half = gates[0].shape[1]
    stack_rows(blocks, rows)
    for t in range(2 * half // TILE):
        which, col = t * TILE // half, t * TILE % half
        gate = jnp.dot(rows[...], gates[which][:, col : col + TILE], preferred_element_type=f32)
        up = jnp.dot(rows[...], ups[which][:, col : col + TILE], preferred_element_type=f32)
        pre_gate[:, t * TILE : (t + 1) * TILE] = gate
        pre_up[:, t * TILE : (t + 1) * TILE] = up
        hidden[:, t * TILE : (t + 1) * TILE] = (gate * jax.nn.sigmoid(gate) * up).astype(bf16)


def hidden_units(blocks, gates, ups):
    width, half = gates[0].shape
    rows = BLOCKS * blocks[0].shape[0]
    return pl.pallas_call(
        hidden_kernel,
        name="hidden_units",
        out_shape=[jax.ShapeDtypeStruct((rows, 2 * half), kind) for kind in (bf16, f32, f32)],
        in_specs=[VMEM] * (BLOCKS + 4),
        out_specs=[VMEM] * 3,
        scratch_shapes=[pltpu.VMEM((rows, width), bf16)],
        compiler_params=pltpu.CompilerParams(vmem_limit_bytes=20 << 20),
        cost_estimate=pl.CostEstimate(flops=8 * rows * width * half, bytes_accessed=8 * width * half, transcendentals=2 * rows * half),
    )(*blocks, *gates, *ups)


def slot_term_kernel(*refs):
    hidden, downs, outs = refs[0], refs[1:3], refs[3:]
    each, width = outs[0].shape
    half = downs[0].shape[0]
    for n in range(width // TILE):
        cols = pl.ds(n * TILE, TILE)
        total = jnp.dot(hidden[:, :half], downs[0][:, cols], preferred_element_type=f32)
        total = total + jnp.dot(hidden[:, half:], downs[1][:, cols], preferred_element_type=f32)
        part = total.astype(bf16)
        for b in range(BLOCKS):
            outs[b][:, cols] = part[b * each : (b + 1) * each]


def slot_terms(hidden, downs):
    rows = hidden.shape[0]
    half, width = downs[0].shape
    return pl.pallas_call(
        slot_term_kernel,
        name="slot_terms",
        out_shape=[jax.ShapeDtypeStruct((rows // BLOCKS, width), bf16)] * BLOCKS,
        in_specs=[VMEM] * 3,
        out_specs=[VMEM] * BLOCKS,
        compiler_params=pltpu.CompilerParams(vmem_limit_bytes=20 << 20),
        cost_estimate=pl.CostEstimate(flops=4 * rows * width * half, bytes_accessed=4 * width * half, transcendentals=0),
    )(hidden, *downs)


def hidden_grad_kernel(*refs):
    blocks, downs = refs[:BLOCKS], refs[BLOCKS : BLOCKS + 2]
    pre_gate, pre_up, gate_grad, up_grad, rows = refs[BLOCKS + 2 :]
    half = downs[0].shape[0]
    stack_rows(blocks, rows)
    for t in range(2 * half // TILE):
        which, row = t * TILE // half, t * TILE % half
        back = lax.dot_general(rows[...], downs[which][row : row + TILE, :], NT, preferred_element_type=f32)
        gate = pre_gate[:, t * TILE : (t + 1) * TILE]
        up = pre_up[:, t * TILE : (t + 1) * TILE]
        squash = jax.nn.sigmoid(gate)
        gate_grad[:, t * TILE : (t + 1) * TILE] = (back * up * squash * (1.0 + gate * (1.0 - squash))).astype(bf16)
        up_grad[:, t * TILE : (t + 1) * TILE] = (back * gate * squash).astype(bf16)


def hidden_grads(blocks, downs, pre_gate, pre_up):
    half, width = downs[0].shape
    rows = pre_gate.shape[0]
    return pl.pallas_call(
        hidden_grad_kernel,
        name="hidden_grads",
        out_shape=[jax.ShapeDtypeStruct((rows, 2 * half), bf16)] * 2,
        in_specs=[VMEM] * (BLOCKS + 4),
        out_specs=[VMEM] * 2,
        scratch_shapes=[pltpu.VMEM((rows, width), bf16)],
        compiler_params=pltpu.CompilerParams(vmem_limit_bytes=20 << 20),
        cost_estimate=pl.CostEstimate(flops=4 * rows * width * half, bytes_accessed=4 * width * half, transcendentals=2 * rows * half),
    )(*blocks, *downs, pre_gate, pre_up)


def slot_grad_kernel(*refs):
    gate_grad, up_grad = refs[:2]
    gates, ups, outs = refs[2:4], refs[4:6], refs[6:]
    each = outs[0].shape[0]
    width, half = gates[0].shape
    for n in range(width // TILE):
        cols = pl.ds(n * TILE, TILE)
        total = None
        for which in range(2):
            for grad, weights in ((gate_grad, gates), (up_grad, ups)):
                term = lax.dot_general(grad[:, which * half : (which + 1) * half], weights[which][cols, :], NT, preferred_element_type=f32)
                total = term if total is None else total + term
        part = total.astype(bf16)
        for b in range(BLOCKS):
            outs[b][:, cols] = part[b * each : (b + 1) * each]


def slot_grads(gate_grad, up_grad, gates, ups):
    width, half = gates[0].shape
    rows = gate_grad.shape[0]
    return pl.pallas_call(
        slot_grad_kernel,
        name="slot_grads",
        out_shape=[jax.ShapeDtypeStruct((rows // BLOCKS, width), bf16)] * BLOCKS,
        in_specs=[VMEM] * 6,
        out_specs=[VMEM] * BLOCKS,
        compiler_params=pltpu.CompilerParams(vmem_limit_bytes=20 << 20),
        cost_estimate=pl.CostEstimate(flops=8 * rows * width * half, bytes_accessed=8 * width * half, transcendentals=0),
    )(gate_grad, up_grad, *gates, *ups)


def three(value):
    high = value.astype(bf16).astype(f32)
    rest = value - high
    mid = rest.astype(bf16).astype(f32)
    return high, mid, rest - mid


SHIFT = 4


def slot_kernel(*refs):
    terms = refs[:4]
    tokens, teacher, aux, langs, base, router, combined_ref, grad_ref, so_far_ref = refs[4:]
    width = tokens.shape[1]
    aux = aux[...]
    gate_value, gate_slope, other = aux[:, 0:1], aux[:, 1:2], aux[:, 2:3]
    total = terms[0][...].astype(f32)
    for t in terms[1:]:
        total = total + t[...].astype(f32)
    combined = tokens[...].astype(f32) + gate_value * total
    combined_ref[...] = combined.astype(bf16)
    deviation = combined - teacher[...].astype(f32)
    grad_ref[:, :width] = (gate_value * deviation).astype(bf16)
    loss = jnp.sum(deviation * deviation, axis=1, keepdims=True) * (0.5 / width)
    dot = jnp.sum(deviation * total, axis=1, keepdims=True) * gate_slope
    lang_sums = base[0:1, :] + jnp.sum(loss * langs[...], axis=0, keepdims=True)
    rows = lax.broadcasted_iota(jnp.int32, langs.shape, 0)
    lanes = lax.broadcasted_iota(jnp.int32, langs.shape, 1)
    extra = jnp.zeros(langs.shape, f32)
    for i, (d, s) in enumerate(zip(three(dot) + (other,), three(lang_sums) + (base[1:2, :],))):
        extra = jnp.where(lanes == i, d, extra)
        extra = jnp.where(jnp.logical_and(rows == i, lanes >= SHIFT), s, extra)
    grad_ref[:, width:] = extra.astype(bf16)
    back = deviation
    columns = lax.broadcasted_iota(jnp.int32, (tokens.shape[0], router.shape[0]), 1)
    direction = (columns == 0).astype(f32) - (columns.astype(f32) == other).astype(f32)
    for part in three(dot):
        back = back + jnp.dot((part * direction).astype(bf16), router[...], preferred_element_type=f32)
    so_far_ref[...] = back


def slots(terms, tokens, teacher, aux, langs, base, router):
    each, width = tokens.shape
    return pl.pallas_call(
        slot_kernel,
        name="slot_step",
        out_shape=[
            jax.ShapeDtypeStruct((each, width), bf16),
            jax.ShapeDtypeStruct((each, width + LANES), bf16),
            jax.ShapeDtypeStruct((each, width), f32),
        ],
        in_specs=[VMEM] * 10,
        out_specs=[VMEM] * 3,
        compiler_params=pltpu.CompilerParams(vmem_limit_bytes=8 << 20),
        cost_estimate=pl.CostEstimate(flops=30 * each * width, bytes_accessed=24 * each * width, transcendentals=0),
    )(*terms, tokens, teacher, aux, langs, base, router)


def router_kernel(*refs):
    token_blocks, grad_blocks = refs[:PLANE], refs[PLANE : 2 * PLANE]
    out, rows = refs[2 * PLANE :]
    experts = out.shape[0]
    width = rows.shape[1]
    stack_rows(token_blocks, rows)
    each = token_blocks[0].shape[0]
    lanes = lax.broadcasted_iota(jnp.int32, (each, LANES), 1)
    expert = lanes % experts
    slopes, langs = [], jnp.zeros((each, LANES), f32)
    for b in range(PLANE):
        extra = grad_blocks[b][:, width:].astype(f32)
        langs = langs + extra
        other = extra[:, 3:4]
        direction = (expert == 0).astype(f32) - (expert.astype(f32) == other).astype(f32)
        part = jnp.where(lanes < experts, extra[:, 0:1], jnp.where(lanes < 2 * experts, extra[:, 1:2], extra[:, 2:3]))
        slopes.append(jnp.where(lanes < 3 * experts, part * direction, 0.0).astype(bf16))
    sums = lax.dot_general(jnp.concatenate(slopes, 0), rows[...], TN, preferred_element_type=f32)
    out[:, :width] = sums[:experts] + sums[experts : 2 * experts] + sums[2 * experts : 3 * experts]
    sub = lax.broadcasted_iota(jnp.int32, (experts, LANES), 0)
    out[:, width:] = jnp.where(sub == 0, langs[0:1] + langs[1:2] + langs[2:3], jnp.where(sub == 1, langs[3:4], 0.0))


def router_sum(token_blocks, grad_blocks, experts):
    each, width = token_blocks[0].shape
    return pl.pallas_call(
        router_kernel,
        name="router_sum",
        out_shape=jax.ShapeDtypeStruct((experts, width + LANES), f32),
        in_specs=[VMEM] * (2 * PLANE),
        out_specs=VMEM,
        scratch_shapes=[pltpu.VMEM((PLANE * each, width), bf16)],
        compiler_params=pltpu.CompilerParams(vmem_limit_bytes=12 << 20),
        cost_estimate=pl.CostEstimate(flops=2 * 128 * 128 * 3072, bytes_accessed=4 * 128 * 3072, transcendentals=0),
    )(*token_blocks, *grad_blocks)


def place_kernel(routes, tokens, placing_ref, slots_ref):
    rows = tokens.shape[0]
    capacity = slots_ref.shape[0]
    chosen = jnp.logical_or(routes[0:1, :] == 0, routes[1:2, :] == 0).astype(f32)
    upper = lax.broadcasted_iota(jnp.int32, (rows, rows), 0) <= lax.broadcasted_iota(jnp.int32, (rows, rows), 1)
    many = jnp.broadcast_to(chosen, (8, rows)).astype(bf16)
    rank = jnp.dot(many, upper.astype(bf16), preferred_element_type=f32)[0:1, :] - 1.0
    slot_ids = lax.broadcasted_iota(jnp.int32, (capacity, rows), 0).astype(f32)
    placing = jnp.where(rank == slot_ids, chosen, 0.0)
    placing_ref[...] = placing
    slots_ref[...] = jnp.dot(placing.astype(bf16), tokens[...], preferred_element_type=f32).astype(bf16)


def place(routes, tokens):
    rows, width = tokens.shape
    return pl.pallas_call(
        place_kernel,
        name="place_tokens",
        out_shape=[jax.ShapeDtypeStruct((rows // 4, rows), f32), jax.ShapeDtypeStruct((rows // 4, width), bf16)],
        in_specs=[VMEM] * 2,
        out_specs=[VMEM] * 2,
        compiler_params=pltpu.CompilerParams(vmem_limit_bytes=8 << 20),
        cost_estimate=pl.CostEstimate(flops=2 * 32 * rows * width, bytes_accessed=3 * rows * width, transcendentals=0),
    )(routes, tokens)


def local(tokens, routes, language, teacher, router_weight, gate_weight, up_weight, down_weight):
    tok_rows, width = tokens.shape
    capacity = tok_rows // 4
    experts = router_weight.shape[1]
    all_tokens = tok_rows * 64
    first_id = routes[:, 0]
    second_id = routes[:, 1]
    chosen = jnp.logical_or(first_id == 0, second_id == 0)
    other_id = jnp.where(first_id == 0, second_id, first_id).astype(f32)
    placing, token_slots = place(routes.T, tokens)
    placing_half = placing.astype(bf16)

    token_blocks = gather(token_slots)
    gates = [gate_weight, twin(after(gate_weight, token_slots))]
    ups = [up_weight, twin(after(up_weight, token_slots))]
    downs = [down_weight, twin(after(down_weight, gates[1], token_blocks[1], token_blocks[2]))]
    tokens, teacher = lax.optimization_barrier((tokens, teacher, token_slots))[:2]

    teacher_slots = jnp.dot(placing_half, teacher, preferred_element_type=f32).astype(bf16)
    logits = jnp.dot(token_slots, router_weight, preferred_element_type=f32)
    other_slots = jnp.sum(placing * other_id[None, :], axis=1)
    filled = jnp.sum(placing, axis=1)
    columns = lax.broadcasted_iota(jnp.int32, logits.shape, 1).astype(f32)
    other_hot = (columns == other_slots[:, None]).astype(f32)
    squash = jax.nn.sigmoid(logits[:, 0] - jnp.sum(logits * other_hot, axis=1))
    gate_value = filled * squash
    gate_slope = filled * squash * (1.0 - squash)
    aux_lane = lax.broadcasted_iota(jnp.int32, (capacity, LANES), 1)
    aux = jnp.where(aux_lane == 0, gate_value[:, None], jnp.where(aux_lane == 1, gate_slope[:, None], other_slots[:, None]))
    plain = tokens.astype(f32) - teacher.astype(f32)
    plain_grad = plain.astype(bf16)
    plain_loss = jnp.where(chosen, 0.0, 0.5 * jnp.mean(plain * plain, axis=1))
    lang_hot = (language[:, None] + SHIFT == lax.broadcasted_iota(jnp.int32, (tok_rows, LANES), 1)).astype(f32)
    slot_langs = jnp.dot(placing_half, lang_hot.astype(bf16), preferred_element_type=f32)
    sub = lax.broadcasted_iota(jnp.int32, (8, LANES), 0)
    base = jnp.where(sub == 0, jnp.sum(plain_loss[:, None] * lang_hot, axis=0)[None, :], jnp.sum(lang_hot, axis=0)[None, :])

    hidden, pre_gate, pre_up = hidden_units(token_blocks, gates, ups)
    terms = slot_terms(hidden, downs)
    combined, grad_slots, so_far = slots(scatter(terms), token_slots, teacher_slots, aux, slot_langs, base, router_weight.T)
    grad_blocks = gather(grad_slots)
    placed = lax.dot_general(placing_half, combined, TN, preferred_element_type=f32)
    layer_out = jnp.where(chosen[:, None], placed.astype(bf16), tokens)

    summed = router_sum(token_blocks[:PLANE], grad_blocks[:PLANE], experts)
    summed = summed + twin(summed)
    gate_grad, up_grad = hidden_grads(grad_blocks, downs, after(pre_gate, summed), pre_up)
    summed = summed + lax.ppermute(summed, "expert", [(i, i ^ 1) for i in range(4)])
    back_terms = slot_grads(after(gate_grad, summed), up_grad, gates, ups)
    summed = summed + lax.ppermute(summed, "expert", [(i, i ^ 2) for i in range(4)])
    summed = summed + pair(summed)
    grad_router = summed[:, :width].T / all_tokens
    lang_loss = (summed[0, width:] / jnp.maximum(summed[1, width:], 1.0))[SHIFT : SHIFT + LANGS]

    own_back = sum(t.astype(f32) for t in scatter(list(back_terms)))
    slot_grad = (so_far + own_back).astype(bf16)
    placed_grad = lax.dot_general(placing_half, slot_grad, TN, preferred_element_type=f32)
    grad_tokens = jnp.where(chosen[:, None], placed_grad.astype(bf16), plain_grad)
    return (layer_out, grad_tokens, grad_router, lang_loss)


def solution(mesh):
    wide = Mesh(mesh.devices.reshape(4, 4, 2, 2, 4), ("expert", "x", "z", "core", "dp"))
    rows = ("dp", "expert", "x", "z", "core")
    hidden = ("x", "z", "core")
    return jax.shard_map(
        local,
        mesh=wide,
        in_specs=(
            P(rows, None),
            P(rows, None),
            P(rows),
            P(rows, None),
            P(),
            P(None, hidden),
            P(None, hidden),
            P(hidden, None),
        ),
        out_specs=(P(rows, None), P(rows, None), P("dp", None), P("dp")),
        check_vma=False,
    )
```

```python
import functools

import jax
import jax.numpy as jnp
from jax import lax
from jax.experimental import pallas as pl
from jax.experimental.pallas import tpu as pltpu
from jax.sharding import Mesh
from jax.sharding import PartitionSpec as P

LANGS = 101
LANES = 128
TILE = 256
BLOCKS = 8
PLANE = 4
NT = (((1,), (1,)), ((), ()))
TN = (((0,), (0,)), ((), ()))
f32 = jnp.float32
bf16 = jnp.bfloat16
GROUP = ("x", "z", "core", "dp")


def move(value, target):
    pairs = []
    for x in range(4):
        for z in range(8):
            for c in range(2):
                tx, tz, tc = target(x, z, c)
                spots = [((px % 4 * 2 + pz % 2) * 2 + pc) * 4 + pz % 8 // 2 for px, pz, pc in ((x, z, c), (tx, tz, tc))]
                pairs.append(tuple(spots))
    return lax.ppermute(value, GROUP, pairs)


def facing(z, c):
    return z + 1 - 2 * ((z + c) % 2)


def ahead(value):
    return move(value, lambda x, z, c: (x + 1 - 2 * c, z, c))


def behind(value):
    return move(value, lambda x, z, c: (x - 1 + 2 * c, z, c))


def across(value):
    return move(value, lambda x, z, c: (x, facing(z, c), c))


def ahead_across(value):
    return move(value, lambda x, z, c: (x + 1 - 2 * c, facing(z, c), c))


def behind_across(value):
    return move(value, lambda x, z, c: (x - 1 + 2 * c, facing(z, c), c))


def twin(value):
    return move(value, lambda x, z, c: (x, z, 1 - c))


def pair(value):
    return move(value, lambda x, z, c: (x, z + 1 - 2 * (z % 2), c))


def after(value, *others):
    return lax.optimization_barrier((value, *others))[0]


def gather(own, *others):
    f1 = ahead(own)
    b1 = behind(own)
    z0 = across(own)
    x2 = ahead(after(f1, *others))
    zf1 = across(f1)
    zb1 = across(b1)
    zx2 = behind_across(b1)
    return [own, f1, b1, x2, z0, zf1, zb1, zx2]


def add(*parts):
    return sum(p.astype(f32) for p in parts).astype(bf16)


def scatter(terms):
    own, f1, b1, x2, z0, zf1, zb1, zx2 = terms
    got_zx2 = ahead_across(zx2)
    got_x2 = behind(x2)
    got_zf1 = across(zf1)
    got_zb1 = across(zb1)
    got_z0 = across(z0)
    got_f1 = behind(add(f1, got_x2, got_zf1))
    got_b1 = ahead(add(b1, got_zb1, got_zx2))
    return [own, got_z0, got_f1, got_b1]


def stack_rows(blocks, rows):
    each, width = blocks[0].shape[0], rows.shape[1]
    for b, block in enumerate(blocks):
        rows[b * each : (b + 1) * each] = block[:, :width]


VMEM = pl.BlockSpec(memory_space=pltpu.VMEM)
HBM = pl.BlockSpec(memory_space=pltpu.HBM)


def hidden_kernel(*refs):
    blocks, gates, ups = refs[:BLOCKS], refs[BLOCKS : BLOCKS + 2], refs[BLOCKS + 2 : BLOCKS + 4]
    hidden, pre_gate, pre_up, rows = refs[BLOCKS + 4 :]
    half = gates[0].shape[1]
    stack_rows(blocks, rows)
    for t in range(2 * half // TILE):
        which, col = t * TILE // half, t * TILE % half
        gate = jnp.dot(rows[...], gates[which][:, col : col + TILE], preferred_element_type=f32)
        up = jnp.dot(rows[...], ups[which][:, col : col + TILE], preferred_element_type=f32)
        pre_gate[:, t * TILE : (t + 1) * TILE] = gate
        pre_up[:, t * TILE : (t + 1) * TILE] = up
        hidden[:, t * TILE : (t + 1) * TILE] = (gate * jax.nn.sigmoid(gate) * up).astype(bf16)


def hidden_units(blocks, gates, ups):
    width, half = gates[0].shape
    rows = BLOCKS * blocks[0].shape[0]
    return pl.pallas_call(
        hidden_kernel,
        name="hidden_units",
        out_shape=[jax.ShapeDtypeStruct((rows, 2 * half), kind) for kind in (bf16, f32, f32)],
        in_specs=[VMEM] * (BLOCKS + 4),
        out_specs=[VMEM] * 3,
        scratch_shapes=[pltpu.VMEM((rows, width), bf16)],
        compiler_params=pltpu.CompilerParams(vmem_limit_bytes=20 << 20),
        cost_estimate=pl.CostEstimate(flops=8 * rows * width * half, bytes_accessed=8 * width * half, transcendentals=2 * rows * half),
    )(*blocks, *gates, *ups)


def slot_term_kernel(*refs):
    hidden, downs, outs = refs[0], refs[1:3], refs[3:]
    each, width = outs[0].shape
    half = downs[0].shape[0]
    for n in range(width // TILE):
        cols = pl.ds(n * TILE, TILE)
        total = jnp.dot(hidden[:, :half], downs[0][:, cols], preferred_element_type=f32)
        total = total + jnp.dot(hidden[:, half:], downs[1][:, cols], preferred_element_type=f32)
        part = total.astype(bf16)
        for b in range(BLOCKS):
            outs[b][:, cols] = part[b * each : (b + 1) * each]


def slot_terms(hidden, downs):
    rows = hidden.shape[0]
    half, width = downs[0].shape
    return pl.pallas_call(
        slot_term_kernel,
        name="slot_terms",
        out_shape=[jax.ShapeDtypeStruct((rows // BLOCKS, width), bf16)] * BLOCKS,
        in_specs=[VMEM] * 3,
        out_specs=[VMEM] * BLOCKS,
        compiler_params=pltpu.CompilerParams(vmem_limit_bytes=20 << 20),
        cost_estimate=pl.CostEstimate(flops=4 * rows * width * half, bytes_accessed=4 * width * half, transcendentals=0),
    )(hidden, *downs)


def hidden_grad_kernel(*refs):
    blocks, downs = refs[:BLOCKS], refs[BLOCKS : BLOCKS + 2]
    pre_gate, pre_up, gate_grad, up_grad, rows = refs[BLOCKS + 2 :]
    half = downs[0].shape[0]
    stack_rows(blocks, rows)
    for t in range(2 * half // TILE):
        which, row = t * TILE // half, t * TILE % half
        back = lax.dot_general(rows[...], downs[which][row : row + TILE, :], NT, preferred_element_type=f32)
        gate = pre_gate[:, t * TILE : (t + 1) * TILE]
        up = pre_up[:, t * TILE : (t + 1) * TILE]
        squash = jax.nn.sigmoid(gate)
        gate_grad[:, t * TILE : (t + 1) * TILE] = (back * up * squash * (1.0 + gate * (1.0 - squash))).astype(bf16)
        up_grad[:, t * TILE : (t + 1) * TILE] = (back * gate * squash).astype(bf16)


def hidden_grads(blocks, downs, pre_gate, pre_up):
    half, width = downs[0].shape
    rows = pre_gate.shape[0]
    return pl.pallas_call(
        hidden_grad_kernel,
        name="hidden_grads",
        out_shape=[jax.ShapeDtypeStruct((rows, 2 * half), bf16)] * 2,
        in_specs=[VMEM] * (BLOCKS + 4),
        out_specs=[VMEM] * 2,
        scratch_shapes=[pltpu.VMEM((rows, width), bf16)],
        compiler_params=pltpu.CompilerParams(vmem_limit_bytes=20 << 20),
        cost_estimate=pl.CostEstimate(flops=4 * rows * width * half, bytes_accessed=4 * width * half, transcendentals=2 * rows * half),
    )(*blocks, *downs, pre_gate, pre_up)


def slot_grad_kernel(*refs):
    gate_grad, up_grad = refs[:2]
    gates, ups, outs = refs[2:4], refs[4:6], refs[6:]
    each = outs[0].shape[0]
    width, half = gates[0].shape
    for n in range(width // TILE):
        cols = pl.ds(n * TILE, TILE)
        total = None
        for which in range(2):
            for grad, weights in ((gate_grad, gates), (up_grad, ups)):
                term = lax.dot_general(grad[:, which * half : (which + 1) * half], weights[which][cols, :], NT, preferred_element_type=f32)
                total = term if total is None else total + term
        part = total.astype(bf16)
        for b in range(BLOCKS):
            outs[b][:, cols] = part[b * each : (b + 1) * each]


def slot_grads(gate_grad, up_grad, gates, ups):
    width, half = gates[0].shape
    rows = gate_grad.shape[0]
    return pl.pallas_call(
        slot_grad_kernel,
        name="slot_grads",
        out_shape=[jax.ShapeDtypeStruct((rows // BLOCKS, width), bf16)] * BLOCKS,
        in_specs=[VMEM] * 6,
        out_specs=[VMEM] * BLOCKS,
        compiler_params=pltpu.CompilerParams(vmem_limit_bytes=20 << 20),
        cost_estimate=pl.CostEstimate(flops=8 * rows * width * half, bytes_accessed=8 * width * half, transcendentals=0),
    )(gate_grad, up_grad, *gates, *ups)


def three(value):
    high = value.astype(bf16).astype(f32)
    rest = value - high
    mid = rest.astype(bf16).astype(f32)
    return high, mid, rest - mid


SHIFT = 4


def slot_kernel(*refs):
    terms = refs[:4]
    tokens, teacher, aux, langs, base, router, combined_ref, grad_ref, so_far_ref = refs[4:]
    width = tokens.shape[1]
    aux = aux[...]
    gate_value, gate_slope, other = aux[:, 0:1], aux[:, 1:2], aux[:, 2:3]
    total = terms[0][...].astype(f32)
    for t in terms[1:]:
        total = total + t[...].astype(f32)
    combined = tokens[...].astype(f32) + gate_value * total
    combined_ref[...] = combined.astype(bf16)
    deviation = combined - teacher[...].astype(f32)
    grad_ref[:, :width] = (gate_value * deviation).astype(bf16)
    loss = jnp.sum(deviation * deviation, axis=1, keepdims=True) * (0.5 / width)
    dot = jnp.sum(deviation * total, axis=1, keepdims=True) * gate_slope
    lang_sums = base[0:1, :] + jnp.sum(loss * langs[...], axis=0, keepdims=True)
    rows = lax.broadcasted_iota(jnp.int32, langs.shape, 0)
    lanes = lax.broadcasted_iota(jnp.int32, langs.shape, 1)
    extra = jnp.zeros(langs.shape, f32)
    for i, (d, s) in enumerate(zip(three(dot) + (other,), three(lang_sums) + (base[1:2, :],))):
        extra = jnp.where(lanes == i, d, extra)
        extra = jnp.where(jnp.logical_and(rows == i, lanes >= SHIFT), s, extra)
    grad_ref[:, width:] = extra.astype(bf16)
    back = deviation
    columns = lax.broadcasted_iota(jnp.int32, (tokens.shape[0], router.shape[0]), 1)
    direction = (columns == 0).astype(f32) - (columns.astype(f32) == other).astype(f32)
    for part in three(dot):
        back = back + jnp.dot((part * direction).astype(bf16), router[...], preferred_element_type=f32)
    so_far_ref[...] = back


def slots(terms, tokens, teacher, aux, langs, base, router):
    each, width = tokens.shape
    return pl.pallas_call(
        slot_kernel,
        name="slot_step",
        out_shape=[
            jax.ShapeDtypeStruct((each, width), bf16),
            jax.ShapeDtypeStruct((each, width + LANES), bf16),
            jax.ShapeDtypeStruct((each, width), f32),
        ],
        in_specs=[VMEM] * 10,
        out_specs=[VMEM] * 3,
        compiler_params=pltpu.CompilerParams(vmem_limit_bytes=8 << 20),
        cost_estimate=pl.CostEstimate(flops=30 * each * width, bytes_accessed=24 * each * width, transcendentals=0),
    )(*terms, tokens, teacher, aux, langs, base, router)


def router_kernel(*refs):
    token_blocks, grad_blocks = refs[:PLANE], refs[PLANE : 2 * PLANE]
    out, rows = refs[2 * PLANE :]
    experts = out.shape[0]
    width = rows.shape[1]
    stack_rows(token_blocks, rows)
    each = token_blocks[0].shape[0]
    lanes = lax.broadcasted_iota(jnp.int32, (each, LANES), 1)
    expert = lanes % experts
    slopes, langs = [], jnp.zeros((each, LANES), f32)
    for b in range(PLANE):
        extra = grad_blocks[b][:, width:].astype(f32)
        langs = langs + extra
        other = extra[:, 3:4]
        direction = (expert == 0).astype(f32) - (expert.astype(f32) == other).astype(f32)
        part = jnp.where(lanes < experts, extra[:, 0:1], jnp.where(lanes < 2 * experts, extra[:, 1:2], extra[:, 2:3]))
        slopes.append(jnp.where(lanes < 3 * experts, part * direction, 0.0).astype(bf16))
    sums = lax.dot_general(jnp.concatenate(slopes, 0), rows[...], TN, preferred_element_type=f32)
    out[:, :width] = sums[:experts] + sums[experts : 2 * experts] + sums[2 * experts : 3 * experts]
    sub = lax.broadcasted_iota(jnp.int32, (experts, LANES), 0)
    out[:, width:] = jnp.where(sub == 0, langs[0:1] + langs[1:2] + langs[2:3], jnp.where(sub == 1, langs[3:4], 0.0))


def router_sum(token_blocks, grad_blocks, experts):
    each, width = token_blocks[0].shape
    return pl.pallas_call(
        router_kernel,
        name="router_sum",
        out_shape=jax.ShapeDtypeStruct((experts, width + LANES), f32),
        in_specs=[VMEM] * (2 * PLANE),
        out_specs=VMEM,
        scratch_shapes=[pltpu.VMEM((PLANE * each, width), bf16)],
        compiler_params=pltpu.CompilerParams(vmem_limit_bytes=12 << 20),
        cost_estimate=pl.CostEstimate(flops=2 * 128 * 128 * 3072, bytes_accessed=4 * 128 * 3072, transcendentals=0),
    )(*token_blocks, *grad_blocks)


def load_kernel(gate, up, gate_ref, up_ref, sems):
    copies = [pltpu.make_async_copy(gate, gate_ref, sems.at[0]), pltpu.make_async_copy(up, up_ref, sems.at[1])]
    for copy in copies:
        copy.start()
    for copy in copies:
        copy.wait()


def load(gate, up):
    return pl.pallas_call(
        load_kernel,
        name="load_weights",
        out_shape=[jax.ShapeDtypeStruct(w.shape, w.dtype) for w in (gate, up)],
        in_specs=[HBM] * 2,
        out_specs=[VMEM] * 2,
        scratch_shapes=[pltpu.SemaphoreType.DMA((2,))],
        compiler_params=pltpu.CompilerParams(vmem_limit_bytes=8 << 20),
        cost_estimate=pl.CostEstimate(flops=0, bytes_accessed=4 * gate.size, transcendentals=0),
    )(gate, up)


def place_kernel(routes, tokens, placing_ref, slots_ref):
    rows = tokens.shape[0]
    capacity = slots_ref.shape[0]
    chosen = jnp.logical_or(routes[0:1, :] == 0, routes[1:2, :] == 0).astype(f32)
    upper = lax.broadcasted_iota(jnp.int32, (rows, rows), 0) <= lax.broadcasted_iota(jnp.int32, (rows, rows), 1)
    many = jnp.broadcast_to(chosen, (8, rows)).astype(bf16)
    rank = jnp.dot(many, upper.astype(bf16), preferred_element_type=f32)[0:1, :] - 1.0
    slot_ids = lax.broadcasted_iota(jnp.int32, (capacity, rows), 0).astype(f32)
    placing = jnp.where(rank == slot_ids, chosen, 0.0)
    placing_ref[...] = placing
    slots_ref[...] = jnp.dot(placing.astype(bf16), tokens[...], preferred_element_type=f32).astype(bf16)


def place(routes, tokens):
    rows, width = tokens.shape
    return pl.pallas_call(
        place_kernel,
        name="place_tokens",
        out_shape=[jax.ShapeDtypeStruct((rows // 4, rows), f32), jax.ShapeDtypeStruct((rows // 4, width), bf16)],
        in_specs=[VMEM] * 2,
        out_specs=[VMEM] * 2,
        compiler_params=pltpu.CompilerParams(vmem_limit_bytes=8 << 20),
        cost_estimate=pl.CostEstimate(flops=2 * 32 * rows * width, bytes_accessed=3 * rows * width, transcendentals=0),
    )(routes, tokens)


def local(tokens, routes, language, teacher, router_weight, gate_weight, up_weight, down_weight):
    tok_rows, width = tokens.shape
    capacity = tok_rows // 4
    experts = router_weight.shape[1]
    all_tokens = tok_rows * 64
    placing, token_slots = place(routes.T, tokens)

    own_gate, own_up = load(after(gate_weight, token_slots), up_weight)
    token_blocks = gather(token_slots, own_gate)
    gates = [own_gate, twin(after(gate_weight, token_slots))]
    ups = [own_up, twin(after(up_weight, token_slots))]
    downs = [down_weight, twin(after(down_weight, *token_blocks[1:]))]
    hidden, pre_gate, pre_up = hidden_units(token_blocks, gates, ups)
    terms = slot_terms(hidden, downs)

    tokens, teacher, routes, language = lax.optimization_barrier((tokens, teacher, routes, language, hidden))[:4]
    first_id = routes[:, 0]
    second_id = routes[:, 1]
    chosen = jnp.logical_or(first_id == 0, second_id == 0)
    other_id = jnp.where(first_id == 0, second_id, first_id).astype(f32)
    placing_half = placing.astype(bf16)
    teacher_slots = jnp.dot(placing_half, teacher, preferred_element_type=f32).astype(bf16)
    logits = jnp.dot(token_slots, router_weight, preferred_element_type=f32)
    other_slots = jnp.sum(placing * other_id[None, :], axis=1)
    filled = jnp.sum(placing, axis=1)
    columns = lax.broadcasted_iota(jnp.int32, logits.shape, 1).astype(f32)
    other_hot = (columns == other_slots[:, None]).astype(f32)
    squash = jax.nn.sigmoid(logits[:, 0] - jnp.sum(logits * other_hot, axis=1))
    gate_value = filled * squash
    gate_slope = filled * squash * (1.0 - squash)
    aux_lane = lax.broadcasted_iota(jnp.int32, (capacity, LANES), 1)
    aux = jnp.where(aux_lane == 0, gate_value[:, None], jnp.where(aux_lane == 1, gate_slope[:, None], other_slots[:, None]))
    plain = tokens.astype(f32) - teacher.astype(f32)
    plain_grad = plain.astype(bf16)
    plain_loss = jnp.where(chosen, 0.0, 0.5 * jnp.mean(plain * plain, axis=1))
    lang_hot = (language[:, None] + SHIFT == lax.broadcasted_iota(jnp.int32, (tok_rows, LANES), 1)).astype(f32)
    slot_langs = jnp.dot(placing_half, lang_hot.astype(bf16), preferred_element_type=f32)
    sub = lax.broadcasted_iota(jnp.int32, (8, LANES), 0)
    base = jnp.where(sub == 0, jnp.sum(plain_loss[:, None] * lang_hot, axis=0)[None, :], jnp.sum(lang_hot, axis=0)[None, :])

    combined, grad_slots, so_far = slots(scatter(terms), token_slots, teacher_slots, aux, slot_langs, base, router_weight.T)
    grad_blocks = gather(grad_slots)
    placed = lax.dot_general(placing_half, combined, TN, preferred_element_type=f32)
    layer_out = jnp.where(chosen[:, None], placed.astype(bf16), tokens)

    summed = router_sum(token_blocks[:PLANE], grad_blocks[:PLANE], experts)
    summed = summed + twin(summed)
    gate_grad, up_grad = hidden_grads(grad_blocks, downs, after(pre_gate, summed), pre_up)
    summed = summed + lax.ppermute(summed, "expert", [(i, i ^ 1) for i in range(4)])
    back_terms = slot_grads(after(gate_grad, summed), up_grad, gates, ups)
    summed = summed + lax.ppermute(summed, "expert", [(i, i ^ 2) for i in range(4)])
    summed = summed + pair(summed)
    grad_router = summed[:, :width].T / all_tokens
    lang_loss = (summed[0, width:] / jnp.maximum(summed[1, width:], 1.0))[SHIFT : SHIFT + LANGS]

    own_back = sum(t.astype(f32) for t in scatter(list(back_terms)))
    slot_grad = (so_far + own_back).astype(bf16)
    placed_grad = lax.dot_general(placing_half, slot_grad, TN, preferred_element_type=f32)
    grad_tokens = jnp.where(chosen[:, None], placed_grad.astype(bf16), plain_grad)
    return (layer_out, grad_tokens, grad_router, lang_loss)


def solution(mesh):
    wide = Mesh(mesh.devices.reshape(4, 4, 2, 2, 4), ("expert", "x", "z", "core", "dp"))
    rows = ("dp", "expert", "x", "z", "core")
    hidden = ("x", "z", "core")
    return jax.shard_map(
        local,
        mesh=wide,
        in_specs=(
            P(rows, None),
            P(rows, None),
            P(rows),
            P(rows, None),
            P(),
            P(None, hidden),
            P(None, hidden),
            P(hidden, None),
        ),
        out_specs=(P(rows, None), P(rows, None), P("dp", None), P("dp")),
        check_vma=False,
    )
```

```python
import functools

import jax
import jax.numpy as jnp
from jax import lax
from jax.experimental import pallas as pl
from jax.experimental.pallas import tpu as pltpu
from jax.sharding import Mesh
from jax.sharding import PartitionSpec as P

LANGS = 101
LANES = 128
TILE = 256
BLOCKS = 8
PLANE = 4
NT = (((1,), (1,)), ((), ()))
TN = (((0,), (0,)), ((), ()))
f32 = jnp.float32
bf16 = jnp.bfloat16
GROUP = ("x", "z", "core", "dp")


def move(value, target):
    pairs = []
    for x in range(4):
        for z in range(8):
            for c in range(2):
                tx, tz, tc = target(x, z, c)
                spots = [((px % 4 * 2 + pz % 2) * 2 + pc) * 4 + pz % 8 // 2 for px, pz, pc in ((x, z, c), (tx, tz, tc))]
                pairs.append(tuple(spots))
    return lax.ppermute(value, GROUP, pairs)


def facing(z, c):
    return z + 1 - 2 * ((z + c) % 2)


def ahead(value):
    return move(value, lambda x, z, c: (x + 1 - 2 * c, z, c))


def behind(value):
    return move(value, lambda x, z, c: (x - 1 + 2 * c, z, c))


def across(value):
    return move(value, lambda x, z, c: (x, facing(z, c), c))


def ahead_across(value):
    return move(value, lambda x, z, c: (x + 1 - 2 * c, facing(z, c), c))


def behind_across(value):
    return move(value, lambda x, z, c: (x - 1 + 2 * c, facing(z, c), c))


def twin(value):
    return move(value, lambda x, z, c: (x, z, 1 - c))


def pair(value):
    return move(value, lambda x, z, c: (x, z + 1 - 2 * (z % 2), c))


def after(value, *others):
    return lax.optimization_barrier((value, *others))[0]


def gather(own, *others):
    f1 = ahead(own)
    b1 = behind(own)
    z0 = across(own)
    f1_late, b1_late = after(f1, *others), after(b1, *others)
    x2 = ahead(f1_late)
    zf1 = across(f1_late)
    zb1 = across(b1_late)
    zx2 = behind_across(b1_late)
    return [own, f1, b1, x2, z0, zf1, zb1, zx2]


def add(*parts):
    return sum(p.astype(f32) for p in parts).astype(bf16)


def scatter(terms):
    own, f1, b1, x2, z0, zf1, zb1, zx2 = terms
    got_zx2 = ahead_across(zx2)
    got_x2 = behind(x2)
    got_zf1 = across(zf1)
    got_zb1 = across(zb1)
    got_z0 = across(after(z0, got_x2))
    got_f1 = behind(add(f1, got_x2, got_zf1))
    got_b1 = ahead(add(b1, got_zb1, got_zx2))
    return [own, got_z0, got_f1, got_b1]


def stack_rows(blocks, rows):
    each, width = blocks[0].shape[0], rows.shape[1]
    for b, block in enumerate(blocks):
        rows[b * each : (b + 1) * each] = block[:, :width]


VMEM = pl.BlockSpec(memory_space=pltpu.VMEM)
HBM = pl.BlockSpec(memory_space=pltpu.HBM)


def hidden_kernel(*refs):
    blocks, gates, ups = refs[:BLOCKS], refs[BLOCKS : BLOCKS + 2], refs[BLOCKS + 2 : BLOCKS + 4]
    hidden, pre_gate, pre_up, rows = refs[BLOCKS + 4 :]
    half = gates[0].shape[1]
    stack_rows(blocks, rows)
    for t in range(2 * half // TILE):
        which, col = t * TILE // half, t * TILE % half
        gate = jnp.dot(rows[...], gates[which][:, col : col + TILE], preferred_element_type=f32)
        up = jnp.dot(rows[...], ups[which][:, col : col + TILE], preferred_element_type=f32)
        pre_gate[:, t * TILE : (t + 1) * TILE] = gate
        pre_up[:, t * TILE : (t + 1) * TILE] = up
        hidden[:, t * TILE : (t + 1) * TILE] = (gate * jax.nn.sigmoid(gate) * up).astype(bf16)


def hidden_units(blocks, gates, ups):
    width, half = gates[0].shape
    rows = BLOCKS * blocks[0].shape[0]
    return pl.pallas_call(
        hidden_kernel,
        name="hidden_units",
        out_shape=[jax.ShapeDtypeStruct((rows, 2 * half), kind) for kind in (bf16, f32, f32)],
        in_specs=[VMEM] * (BLOCKS + 4),
        out_specs=[VMEM] * 3,
        scratch_shapes=[pltpu.VMEM((rows, width), bf16)],
        compiler_params=pltpu.CompilerParams(vmem_limit_bytes=20 << 20),
        cost_estimate=pl.CostEstimate(flops=8 * rows * width * half, bytes_accessed=8 * width * half, transcendentals=2 * rows * half),
    )(*blocks, *gates, *ups)


def slot_term_kernel(*refs):
    hidden, downs, outs = refs[0], refs[1:3], refs[3:]
    each, width = outs[0].shape
    half = downs[0].shape[0]
    for n in range(width // TILE):
        cols = pl.ds(n * TILE, TILE)
        total = jnp.dot(hidden[:, :half], downs[0][:, cols], preferred_element_type=f32)
        total = total + jnp.dot(hidden[:, half:], downs[1][:, cols], preferred_element_type=f32)
        part = total.astype(bf16)
        for b in range(BLOCKS):
            outs[b][:, cols] = part[b * each : (b + 1) * each]


def slot_terms(hidden, downs):
    rows = hidden.shape[0]
    half, width = downs[0].shape
    return pl.pallas_call(
        slot_term_kernel,
        name="slot_terms",
        out_shape=[jax.ShapeDtypeStruct((rows // BLOCKS, width), bf16)] * BLOCKS,
        in_specs=[VMEM] * 3,
        out_specs=[VMEM] * BLOCKS,
        compiler_params=pltpu.CompilerParams(vmem_limit_bytes=20 << 20),
        cost_estimate=pl.CostEstimate(flops=4 * rows * width * half, bytes_accessed=4 * width * half, transcendentals=0),
    )(hidden, *downs)


def hidden_grad_kernel(*refs):
    blocks, downs = refs[:BLOCKS], refs[BLOCKS : BLOCKS + 2]
    pre_gate, pre_up, gate_grad, up_grad, rows = refs[BLOCKS + 2 :]
    half = downs[0].shape[0]
    stack_rows(blocks, rows)
    for t in range(2 * half // TILE):
        which, row = t * TILE // half, t * TILE % half
        back = lax.dot_general(rows[...], downs[which][row : row + TILE, :], NT, preferred_element_type=f32)
        gate = pre_gate[:, t * TILE : (t + 1) * TILE]
        up = pre_up[:, t * TILE : (t + 1) * TILE]
        squash = jax.nn.sigmoid(gate)
        gate_grad[:, t * TILE : (t + 1) * TILE] = (back * up * squash * (1.0 + gate * (1.0 - squash))).astype(bf16)
        up_grad[:, t * TILE : (t + 1) * TILE] = (back * gate * squash).astype(bf16)


def hidden_grads(blocks, downs, pre_gate, pre_up):
    half, width = downs[0].shape
    rows = pre_gate.shape[0]
    return pl.pallas_call(
        hidden_grad_kernel,
        name="hidden_grads",
        out_shape=[jax.ShapeDtypeStruct((rows, 2 * half), bf16)] * 2,
        in_specs=[VMEM] * (BLOCKS + 4),
        out_specs=[VMEM] * 2,
        scratch_shapes=[pltpu.VMEM((rows, width), bf16)],
        compiler_params=pltpu.CompilerParams(vmem_limit_bytes=20 << 20),
        cost_estimate=pl.CostEstimate(flops=4 * rows * width * half, bytes_accessed=4 * width * half, transcendentals=2 * rows * half),
    )(*blocks, *downs, pre_gate, pre_up)


def slot_grad_kernel(*refs):
    gate_grad, up_grad = refs[:2]
    gates, ups, outs = refs[2:4], refs[4:6], refs[6:]
    each = outs[0].shape[0]
    width, half = gates[0].shape
    for n in range(width // TILE):
        cols = pl.ds(n * TILE, TILE)
        total = None
        for which in range(2):
            for grad, weights in ((gate_grad, gates), (up_grad, ups)):
                term = lax.dot_general(grad[:, which * half : (which + 1) * half], weights[which][cols, :], NT, preferred_element_type=f32)
                total = term if total is None else total + term
        part = total.astype(bf16)
        for b in range(BLOCKS):
            outs[b][:, cols] = part[b * each : (b + 1) * each]


def slot_grads(gate_grad, up_grad, gates, ups):
    width, half = gates[0].shape
    rows = gate_grad.shape[0]
    return pl.pallas_call(
        slot_grad_kernel,
        name="slot_grads",
        out_shape=[jax.ShapeDtypeStruct((rows // BLOCKS, width), bf16)] * BLOCKS,
        in_specs=[VMEM] * 6,
        out_specs=[VMEM] * BLOCKS,
        compiler_params=pltpu.CompilerParams(vmem_limit_bytes=20 << 20),
        cost_estimate=pl.CostEstimate(flops=8 * rows * width * half, bytes_accessed=8 * width * half, transcendentals=0),
    )(gate_grad, up_grad, *gates, *ups)


def three(value):
    high = value.astype(bf16).astype(f32)
    rest = value - high
    mid = rest.astype(bf16).astype(f32)
    return high, mid, rest - mid


SHIFT = 4


def slot_kernel(*refs):
    terms = refs[:4]
    tokens, teacher, aux, langs, base, router, combined_ref, grad_ref, so_far_ref = refs[4:]
    width = tokens.shape[1]
    aux = aux[...]
    gate_value, gate_slope, other = aux[:, 0:1], aux[:, 1:2], aux[:, 2:3]
    total = terms[0][...].astype(f32)
    for t in terms[1:]:
        total = total + t[...].astype(f32)
    combined = tokens[...].astype(f32) + gate_value * total
    combined_ref[...] = combined.astype(bf16)
    deviation = combined - teacher[...].astype(f32)
    grad_ref[:, :width] = (gate_value * deviation).astype(bf16)
    loss = jnp.sum(deviation * deviation, axis=1, keepdims=True) * (0.5 / width)
    dot = jnp.sum(deviation * total, axis=1, keepdims=True) * gate_slope
    lang_sums = base[0:1, :] + jnp.sum(loss * langs[...], axis=0, keepdims=True)
    rows = lax.broadcasted_iota(jnp.int32, langs.shape, 0)
    lanes = lax.broadcasted_iota(jnp.int32, langs.shape, 1)
    extra = jnp.zeros(langs.shape, f32)
    for i, (d, s) in enumerate(zip(three(dot) + (other,), three(lang_sums) + (base[1:2, :],))):
        extra = jnp.where(lanes == i, d, extra)
        extra = jnp.where(jnp.logical_and(rows == i, lanes >= SHIFT), s, extra)
    grad_ref[:, width:] = extra.astype(bf16)
    back = deviation
    columns = lax.broadcasted_iota(jnp.int32, (tokens.shape[0], router.shape[0]), 1)
    direction = (columns == 0).astype(f32) - (columns.astype(f32) == other).astype(f32)
    for part in three(dot):
        back = back + jnp.dot((part * direction).astype(bf16), router[...], preferred_element_type=f32)
    so_far_ref[...] = back


def slots(terms, tokens, teacher, aux, langs, base, router):
    each, width = tokens.shape
    return pl.pallas_call(
        slot_kernel,
        name="slot_step",
        out_shape=[
            jax.ShapeDtypeStruct((each, width), bf16),
            jax.ShapeDtypeStruct((each, width + LANES), bf16),
            jax.ShapeDtypeStruct((each, width), f32),
        ],
        in_specs=[VMEM] * 10,
        out_specs=[VMEM] * 3,
        compiler_params=pltpu.CompilerParams(vmem_limit_bytes=8 << 20),
        cost_estimate=pl.CostEstimate(flops=30 * each * width, bytes_accessed=24 * each * width, transcendentals=0),
    )(*terms, tokens, teacher, aux, langs, base, router)


def router_kernel(*refs):
    token_blocks, grad_blocks = refs[:PLANE], refs[PLANE : 2 * PLANE]
    out, rows = refs[2 * PLANE :]
    experts = out.shape[0]
    width = rows.shape[1]
    stack_rows(token_blocks, rows)
    each = token_blocks[0].shape[0]
    lanes = lax.broadcasted_iota(jnp.int32, (each, LANES), 1)
    expert = lanes % experts
    slopes, langs = [], jnp.zeros((each, LANES), f32)
    for b in range(PLANE):
        extra = grad_blocks[b][:, width:].astype(f32)
        langs = langs + extra
        other = extra[:, 3:4]
        direction = (expert == 0).astype(f32) - (expert.astype(f32) == other).astype(f32)
        part = jnp.where(lanes < experts, extra[:, 0:1], jnp.where(lanes < 2 * experts, extra[:, 1:2], extra[:, 2:3]))
        slopes.append(jnp.where(lanes < 3 * experts, part * direction, 0.0).astype(bf16))
    sums = lax.dot_general(jnp.concatenate(slopes, 0), rows[...], TN, preferred_element_type=f32)
    out[:, :width] = sums[:experts] + sums[experts : 2 * experts] + sums[2 * experts : 3 * experts]
    sub = lax.broadcasted_iota(jnp.int32, (experts, LANES), 0)
    out[:, width:] = jnp.where(sub == 0, langs[0:1] + langs[1:2] + langs[2:3], jnp.where(sub == 1, langs[3:4], 0.0))


def router_sum(token_blocks, grad_blocks, experts):
    each, width = token_blocks[0].shape
    return pl.pallas_call(
        router_kernel,
        name="router_sum",
        out_shape=jax.ShapeDtypeStruct((experts, width + LANES), f32),
        in_specs=[VMEM] * (2 * PLANE),
        out_specs=VMEM,
        scratch_shapes=[pltpu.VMEM((PLANE * each, width), bf16)],
        compiler_params=pltpu.CompilerParams(vmem_limit_bytes=12 << 20),
        cost_estimate=pl.CostEstimate(flops=2 * 128 * 128 * 3072, bytes_accessed=4 * 128 * 3072, transcendentals=0),
    )(*token_blocks, *grad_blocks)


def load_kernel(gate, up, gate_ref, up_ref, sems):
    copies = [pltpu.make_async_copy(gate, gate_ref, sems.at[0]), pltpu.make_async_copy(up, up_ref, sems.at[1])]
    for copy in copies:
        copy.start()
    for copy in copies:
        copy.wait()


def load(gate, up):
    return pl.pallas_call(
        load_kernel,
        name="load_weights",
        out_shape=[jax.ShapeDtypeStruct(w.shape, w.dtype) for w in (gate, up)],
        in_specs=[HBM] * 2,
        out_specs=[VMEM] * 2,
        scratch_shapes=[pltpu.SemaphoreType.DMA((2,))],
        compiler_params=pltpu.CompilerParams(vmem_limit_bytes=8 << 20),
        cost_estimate=pl.CostEstimate(flops=0, bytes_accessed=4 * gate.size, transcendentals=0),
    )(gate, up)


def place_kernel(routes, tokens, placing_ref, slots_ref):
    rows = tokens.shape[0]
    capacity = slots_ref.shape[0]
    chosen = jnp.logical_or(routes[0:1, :] == 0, routes[1:2, :] == 0).astype(f32)
    upper = lax.broadcasted_iota(jnp.int32, (rows, rows), 0) <= lax.broadcasted_iota(jnp.int32, (rows, rows), 1)
    many = jnp.broadcast_to(chosen, (8, rows)).astype(bf16)
    rank = jnp.dot(many, upper.astype(bf16), preferred_element_type=f32)[0:1, :] - 1.0
    slot_ids = lax.broadcasted_iota(jnp.int32, (capacity, rows), 0).astype(f32)
    placing = jnp.where(rank == slot_ids, chosen, 0.0)
    placing_ref[...] = placing
    slots_ref[...] = jnp.dot(placing.astype(bf16), tokens[...], preferred_element_type=f32).astype(bf16)


def place(routes, tokens):
    rows, width = tokens.shape
    return pl.pallas_call(
        place_kernel,
        name="place_tokens",
        out_shape=[jax.ShapeDtypeStruct((rows // 4, rows), f32), jax.ShapeDtypeStruct((rows // 4, width), bf16)],
        in_specs=[VMEM] * 2,
        out_specs=[VMEM] * 2,
        compiler_params=pltpu.CompilerParams(vmem_limit_bytes=8 << 20),
        cost_estimate=pl.CostEstimate(flops=2 * 32 * rows * width, bytes_accessed=3 * rows * width, transcendentals=0),
    )(routes, tokens)


def local(tokens, routes, language, teacher, router_weight, gate_weight, up_weight, down_weight):
    tok_rows, width = tokens.shape
    capacity = tok_rows // 4
    experts = router_weight.shape[1]
    all_tokens = tok_rows * 64
    placing, token_slots = place(routes.T, tokens)

    own_gate, own_up = load(after(gate_weight, token_slots), up_weight)
    token_blocks = gather(token_slots, own_gate)
    gates = [own_gate, twin(after(gate_weight, token_slots))]
    ups = [own_up, twin(after(up_weight, token_slots))]
    downs = [down_weight, twin(after(down_weight, *token_blocks[1:]))]
    hidden, pre_gate, pre_up = hidden_units(token_blocks, gates, ups)
    terms = slot_terms(hidden, downs)

    tokens, teacher, routes, language = lax.optimization_barrier((tokens, teacher, routes, language, hidden))[:4]
    first_id = routes[:, 0]
    second_id = routes[:, 1]
    chosen = jnp.logical_or(first_id == 0, second_id == 0)
    other_id = jnp.where(first_id == 0, second_id, first_id).astype(f32)
    placing_half = placing.astype(bf16)
    teacher_slots = jnp.dot(placing_half, teacher, preferred_element_type=f32).astype(bf16)
    logits = jnp.dot(token_slots, router_weight, preferred_element_type=f32)
    other_slots = jnp.sum(placing * other_id[None, :], axis=1)
    filled = jnp.sum(placing, axis=1)
    columns = lax.broadcasted_iota(jnp.int32, logits.shape, 1).astype(f32)
    other_hot = (columns == other_slots[:, None]).astype(f32)
    squash = jax.nn.sigmoid(logits[:, 0] - jnp.sum(logits * other_hot, axis=1))
    gate_value = filled * squash
    gate_slope = filled * squash * (1.0 - squash)
    aux_lane = lax.broadcasted_iota(jnp.int32, (capacity, LANES), 1)
    aux = jnp.where(aux_lane == 0, gate_value[:, None], jnp.where(aux_lane == 1, gate_slope[:, None], other_slots[:, None]))
    plain = tokens.astype(f32) - teacher.astype(f32)
    plain_grad = plain.astype(bf16)
    plain_loss = jnp.where(chosen, 0.0, 0.5 * jnp.mean(plain * plain, axis=1))
    lang_hot = (language[:, None] + SHIFT == lax.broadcasted_iota(jnp.int32, (tok_rows, LANES), 1)).astype(f32)
    slot_langs = jnp.dot(placing_half, lang_hot.astype(bf16), preferred_element_type=f32)
    sub = lax.broadcasted_iota(jnp.int32, (8, LANES), 0)
    base = jnp.where(sub == 0, jnp.sum(plain_loss[:, None] * lang_hot, axis=0)[None, :], jnp.sum(lang_hot, axis=0)[None, :])

    combined, grad_slots, so_far = slots(scatter(terms), token_slots, teacher_slots, aux, slot_langs, base, router_weight.T)
    placed = lax.dot_general(placing_half, combined, TN, preferred_element_type=f32)
    layer_out = jnp.where(chosen[:, None], placed.astype(bf16), tokens)
    grad_blocks = gather(grad_slots, layer_out)

    summed = router_sum(token_blocks[:PLANE], grad_blocks[:PLANE], experts)
    summed = summed + twin(summed)
    gate_grad, up_grad = hidden_grads(grad_blocks, downs, after(pre_gate, summed), pre_up)
    summed = summed + lax.ppermute(summed, "expert", [(i, i ^ 1) for i in range(4)])
    back_terms = slot_grads(after(gate_grad, summed), up_grad, gates, ups)
    summed = summed + lax.ppermute(summed, "expert", [(i, i ^ 2) for i in range(4)])
    summed = summed + pair(summed)
    grad_router = summed[:, :width].T / all_tokens
    lang_loss = (summed[0, width:] / jnp.maximum(summed[1, width:], 1.0))[SHIFT : SHIFT + LANGS]

    own_back = sum(t.astype(f32) for t in scatter(list(back_terms)))
    slot_grad = (so_far + own_back).astype(bf16)
    placed_grad = lax.dot_general(placing_half, slot_grad, TN, preferred_element_type=f32)
    grad_tokens = jnp.where(chosen[:, None], placed_grad.astype(bf16), plain_grad)
    return (layer_out, grad_tokens, grad_router, lang_loss)


def solution(mesh):
    wide = Mesh(mesh.devices.reshape(4, 4, 2, 2, 4), ("expert", "x", "z", "core", "dp"))
    rows = ("dp", "expert", "x", "z", "core")
    hidden = ("x", "z", "core")
    return jax.shard_map(
        local,
        mesh=wide,
        in_specs=(
            P(rows, None),
            P(rows, None),
            P(rows),
            P(rows, None),
            P(),
            P(None, hidden),
            P(None, hidden),
            P(hidden, None),
        ),
        out_specs=(P(rows, None), P(rows, None), P("dp", None), P("dp")),
        check_vma=False,
    )
```

```python
import functools

import jax
import jax.numpy as jnp
from jax import lax
from jax.experimental import pallas as pl
from jax.experimental.pallas import tpu as pltpu
from jax.sharding import Mesh
from jax.sharding import PartitionSpec as P

LANGS = 101
LANES = 128
TILE = 256
BLOCKS = 8
PLANE = 4
NT = (((1,), (1,)), ((), ()))
TN = (((0,), (0,)), ((), ()))
f32 = jnp.float32
bf16 = jnp.bfloat16
GROUP = ("x", "z", "core", "dp")


def move(value, target):
    pairs = []
    for x in range(4):
        for z in range(8):
            for c in range(2):
                tx, tz, tc = target(x, z, c)
                spots = [((px % 4 * 2 + pz % 2) * 2 + pc) * 4 + pz % 8 // 2 for px, pz, pc in ((x, z, c), (tx, tz, tc))]
                pairs.append(tuple(spots))
    return lax.ppermute(value, GROUP, pairs)


def facing(z, c):
    return z + 1 - 2 * ((z + c) % 2)


def ahead(value):
    return move(value, lambda x, z, c: (x + 1 - 2 * c, z, c))


def behind(value):
    return move(value, lambda x, z, c: (x - 1 + 2 * c, z, c))


def across(value):
    return move(value, lambda x, z, c: (x, facing(z, c), c))


def ahead_across(value):
    return move(value, lambda x, z, c: (x + 1 - 2 * c, facing(z, c), c))


def behind_across(value):
    return move(value, lambda x, z, c: (x - 1 + 2 * c, facing(z, c), c))


def twin(value):
    return move(value, lambda x, z, c: (x, z, 1 - c))


def pair(value):
    return move(value, lambda x, z, c: (x, z + 1 - 2 * (z % 2), c))


def after(value, *others):
    return lax.optimization_barrier((value, *others))[0]


def gather(own, early, *late):
    f1 = ahead(own)
    b1 = behind(own)
    z0 = across(own)
    f1_late, b1_late = after(f1, early, *late), after(b1, early)
    x2 = ahead(f1_late)
    zf1 = across(f1_late)
    zb1 = across(b1_late)
    zx2 = behind_across(b1_late)
    return [own, f1, b1, x2, z0, zf1, zb1, zx2]


def add(*parts):
    return sum(p.astype(f32) for p in parts).astype(bf16)


def scatter(terms):
    own, f1, b1, x2, z0, zf1, zb1, zx2 = terms
    got_zx2 = ahead_across(zx2)
    got_x2 = behind(x2)
    got_zf1 = across(zf1)
    got_zb1 = across(zb1)
    got_z0 = across(after(z0, got_x2))
    got_f1 = behind(add(f1, got_x2, got_zf1))
    got_b1 = ahead(add(b1, got_zb1, got_zx2))
    return [own, got_z0, got_f1, got_b1]


def stack_rows(blocks, rows):
    each, width = blocks[0].shape[0], rows.shape[1]
    for b, block in enumerate(blocks):
        rows[b * each : (b + 1) * each] = block[:, :width]


VMEM = pl.BlockSpec(memory_space=pltpu.VMEM)
HBM = pl.BlockSpec(memory_space=pltpu.HBM)


def hidden_kernel(*refs):
    blocks, gates, ups = refs[:BLOCKS], refs[BLOCKS : BLOCKS + 2], refs[BLOCKS + 2 : BLOCKS + 4]
    hidden, pre_gate, pre_up, rows = refs[BLOCKS + 4 :]
    half = gates[0].shape[1]
    stack_rows(blocks, rows)
    for t in range(2 * half // TILE):
        which, col = t * TILE // half, t * TILE % half
        gate = jnp.dot(rows[...], gates[which][:, col : col + TILE], preferred_element_type=f32)
        up = jnp.dot(rows[...], ups[which][:, col : col + TILE], preferred_element_type=f32)
        pre_gate[:, t * TILE : (t + 1) * TILE] = gate
        pre_up[:, t * TILE : (t + 1) * TILE] = up
        hidden[:, t * TILE : (t + 1) * TILE] = (gate * jax.nn.sigmoid(gate) * up).astype(bf16)


def hidden_units(blocks, gates, ups):
    width, half = gates[0].shape
    rows = BLOCKS * blocks[0].shape[0]
    return pl.pallas_call(
        hidden_kernel,
        name="hidden_units",
        out_shape=[jax.ShapeDtypeStruct((rows, 2 * half), kind) for kind in (bf16, f32, f32)],
        in_specs=[VMEM] * (BLOCKS + 4),
        out_specs=[VMEM] * 3,
        scratch_shapes=[pltpu.VMEM((rows, width), bf16)],
        compiler_params=pltpu.CompilerParams(vmem_limit_bytes=20 << 20),
        cost_estimate=pl.CostEstimate(flops=8 * rows * width * half, bytes_accessed=8 * width * half, transcendentals=2 * rows * half),
    )(*blocks, *gates, *ups)


def slot_term_kernel(*refs):
    hidden, downs, outs = refs[0], refs[1:3], refs[3:]
    each, width = outs[0].shape
    half = downs[0].shape[0]
    for n in range(width // TILE):
        cols = pl.ds(n * TILE, TILE)
        total = jnp.dot(hidden[:, :half], downs[0][:, cols], preferred_element_type=f32)
        total = total + jnp.dot(hidden[:, half:], downs[1][:, cols], preferred_element_type=f32)
        part = total.astype(bf16)
        for b in range(BLOCKS):
            outs[b][:, cols] = part[b * each : (b + 1) * each]


def slot_terms(hidden, downs):
    rows = hidden.shape[0]
    half, width = downs[0].shape
    return pl.pallas_call(
        slot_term_kernel,
        name="slot_terms",
        out_shape=[jax.ShapeDtypeStruct((rows // BLOCKS, width), bf16)] * BLOCKS,
        in_specs=[VMEM] * 3,
        out_specs=[VMEM] * BLOCKS,
        compiler_params=pltpu.CompilerParams(vmem_limit_bytes=20 << 20),
        cost_estimate=pl.CostEstimate(flops=4 * rows * width * half, bytes_accessed=4 * width * half, transcendentals=0),
    )(hidden, *downs)


def hidden_grad_kernel(*refs):
    blocks, downs = refs[:BLOCKS], refs[BLOCKS : BLOCKS + 2]
    pre_gate, pre_up, gate_grad, up_grad, rows = refs[BLOCKS + 2 :]
    half = downs[0].shape[0]
    stack_rows(blocks, rows)
    for t in range(2 * half // TILE):
        which, row = t * TILE // half, t * TILE % half
        back = lax.dot_general(rows[...], downs[which][row : row + TILE, :], NT, preferred_element_type=f32)
        gate = pre_gate[:, t * TILE : (t + 1) * TILE]
        up = pre_up[:, t * TILE : (t + 1) * TILE]
        squash = jax.nn.sigmoid(gate)
        gate_grad[:, t * TILE : (t + 1) * TILE] = (back * up * squash * (1.0 + gate * (1.0 - squash))).astype(bf16)
        up_grad[:, t * TILE : (t + 1) * TILE] = (back * gate * squash).astype(bf16)


def hidden_grads(blocks, downs, pre_gate, pre_up):
    half, width = downs[0].shape
    rows = pre_gate.shape[0]
    return pl.pallas_call(
        hidden_grad_kernel,
        name="hidden_grads",
        out_shape=[jax.ShapeDtypeStruct((rows, 2 * half), bf16)] * 2,
        in_specs=[VMEM] * (BLOCKS + 4),
        out_specs=[VMEM] * 2,
        scratch_shapes=[pltpu.VMEM((rows, width), bf16)],
        compiler_params=pltpu.CompilerParams(vmem_limit_bytes=20 << 20),
        cost_estimate=pl.CostEstimate(flops=4 * rows * width * half, bytes_accessed=4 * width * half, transcendentals=2 * rows * half),
    )(*blocks, *downs, pre_gate, pre_up)


def slot_grad_kernel(*refs):
    gate_grad, up_grad = refs[:2]
    gates, ups, outs = refs[2:4], refs[4:6], refs[6:]
    each = outs[0].shape[0]
    width, half = gates[0].shape
    for n in range(width // TILE):
        cols = pl.ds(n * TILE, TILE)
        total = None
        for which in range(2):
            for grad, weights in ((gate_grad, gates), (up_grad, ups)):
                term = lax.dot_general(grad[:, which * half : (which + 1) * half], weights[which][cols, :], NT, preferred_element_type=f32)
                total = term if total is None else total + term
        part = total.astype(bf16)
        for b in range(BLOCKS):
            outs[b][:, cols] = part[b * each : (b + 1) * each]


def slot_grads(gate_grad, up_grad, gates, ups):
    width, half = gates[0].shape
    rows = gate_grad.shape[0]
    return pl.pallas_call(
        slot_grad_kernel,
        name="slot_grads",
        out_shape=[jax.ShapeDtypeStruct((rows // BLOCKS, width), bf16)] * BLOCKS,
        in_specs=[VMEM] * 6,
        out_specs=[VMEM] * BLOCKS,
        compiler_params=pltpu.CompilerParams(vmem_limit_bytes=20 << 20),
        cost_estimate=pl.CostEstimate(flops=8 * rows * width * half, bytes_accessed=8 * width * half, transcendentals=0),
    )(gate_grad, up_grad, *gates, *ups)


def three(value):
    high = value.astype(bf16).astype(f32)
    rest = value - high
    mid = rest.astype(bf16).astype(f32)
    return high, mid, rest - mid


SHIFT = 4


def slot_kernel(*refs):
    terms = refs[:4]
    tokens, teacher, aux, langs, base, router, combined_ref, grad_ref, so_far_ref = refs[4:]
    width = tokens.shape[1]
    aux = aux[...]
    gate_value, gate_slope, other = aux[:, 0:1], aux[:, 1:2], aux[:, 2:3]
    total = terms[0][...].astype(f32)
    for t in terms[1:]:
        total = total + t[...].astype(f32)
    combined = tokens[...].astype(f32) + gate_value * total
    combined_ref[...] = combined.astype(bf16)
    deviation = combined - teacher[...].astype(f32)
    grad_ref[:, :width] = (gate_value * deviation).astype(bf16)
    loss = jnp.sum(deviation * deviation, axis=1, keepdims=True) * (0.5 / width)
    dot = jnp.sum(deviation * total, axis=1, keepdims=True) * gate_slope
    lang_sums = base[0:1, :] + jnp.sum(loss * langs[...], axis=0, keepdims=True)
    rows = lax.broadcasted_iota(jnp.int32, langs.shape, 0)
    lanes = lax.broadcasted_iota(jnp.int32, langs.shape, 1)
    extra = jnp.zeros(langs.shape, f32)
    for i, (d, s) in enumerate(zip(three(dot) + (other,), three(lang_sums) + (base[1:2, :],))):
        extra = jnp.where(lanes == i, d, extra)
        extra = jnp.where(jnp.logical_and(rows == i, lanes >= SHIFT), s, extra)
    grad_ref[:, width:] = extra.astype(bf16)
    back = deviation
    columns = lax.broadcasted_iota(jnp.int32, (tokens.shape[0], router.shape[0]), 1)
    direction = (columns == 0).astype(f32) - (columns.astype(f32) == other).astype(f32)
    for part in three(dot):
        back = back + jnp.dot((part * direction).astype(bf16), router[...], preferred_element_type=f32)
    so_far_ref[...] = back


def slots(terms, tokens, teacher, aux, langs, base, router):
    each, width = tokens.shape
    return pl.pallas_call(
        slot_kernel,
        name="slot_step",
        out_shape=[
            jax.ShapeDtypeStruct((each, width), bf16),
            jax.ShapeDtypeStruct((each, width + LANES), bf16),
            jax.ShapeDtypeStruct((each, width), f32),
        ],
        in_specs=[VMEM] * 10,
        out_specs=[VMEM] * 3,
        compiler_params=pltpu.CompilerParams(vmem_limit_bytes=8 << 20),
        cost_estimate=pl.CostEstimate(flops=30 * each * width, bytes_accessed=24 * each * width, transcendentals=0),
    )(*terms, tokens, teacher, aux, langs, base, router)


def router_kernel(*refs):
    token_blocks, grad_blocks = refs[:PLANE], refs[PLANE : 2 * PLANE]
    out, rows = refs[2 * PLANE :]
    experts = out.shape[0]
    width = rows.shape[1]
    stack_rows(token_blocks, rows)
    each = token_blocks[0].shape[0]
    lanes = lax.broadcasted_iota(jnp.int32, (each, LANES), 1)
    expert = lanes % experts
    slopes, langs = [], jnp.zeros((each, LANES), f32)
    for b in range(PLANE):
        extra = grad_blocks[b][:, width:].astype(f32)
        langs = langs + extra
        other = extra[:, 3:4]
        direction = (expert == 0).astype(f32) - (expert.astype(f32) == other).astype(f32)
        part = jnp.where(lanes < experts, extra[:, 0:1], jnp.where(lanes < 2 * experts, extra[:, 1:2], extra[:, 2:3]))
        slopes.append(jnp.where(lanes < 3 * experts, part * direction, 0.0).astype(bf16))
    sums = lax.dot_general(jnp.concatenate(slopes, 0), rows[...], TN, preferred_element_type=f32)
    out[:, :width] = sums[:experts] + sums[experts : 2 * experts] + sums[2 * experts : 3 * experts]
    sub = lax.broadcasted_iota(jnp.int32, (experts, LANES), 0)
    out[:, width:] = jnp.where(sub == 0, langs[0:1] + langs[1:2] + langs[2:3], jnp.where(sub == 1, langs[3:4], 0.0))


def router_sum(token_blocks, grad_blocks, experts):
    each, width = token_blocks[0].shape
    return pl.pallas_call(
        router_kernel,
        name="router_sum",
        out_shape=jax.ShapeDtypeStruct((experts, width + LANES), f32),
        in_specs=[VMEM] * (2 * PLANE),
        out_specs=VMEM,
        scratch_shapes=[pltpu.VMEM((PLANE * each, width), bf16)],
        compiler_params=pltpu.CompilerParams(vmem_limit_bytes=12 << 20),
        cost_estimate=pl.CostEstimate(flops=2 * 128 * 128 * 3072, bytes_accessed=4 * 128 * 3072, transcendentals=0),
    )(*token_blocks, *grad_blocks)


def load_kernel(gate, up, gate_ref, up_ref, sems):
    copies = [pltpu.make_async_copy(gate, gate_ref, sems.at[0]), pltpu.make_async_copy(up, up_ref, sems.at[1])]
    for copy in copies:
        copy.start()
    for copy in copies:
        copy.wait()


def load(gate, up):
    return pl.pallas_call(
        load_kernel,
        name="load_weights",
        out_shape=[jax.ShapeDtypeStruct(w.shape, w.dtype) for w in (gate, up)],
        in_specs=[HBM] * 2,
        out_specs=[VMEM] * 2,
        scratch_shapes=[pltpu.SemaphoreType.DMA((2,))],
        compiler_params=pltpu.CompilerParams(vmem_limit_bytes=8 << 20),
        cost_estimate=pl.CostEstimate(flops=0, bytes_accessed=4 * gate.size, transcendentals=0),
    )(gate, up)


def place_kernel(routes, tokens, placing_ref, slots_ref):
    rows = tokens.shape[0]
    capacity = slots_ref.shape[0]
    chosen = jnp.logical_or(routes[0:1, :] == 0, routes[1:2, :] == 0).astype(f32)
    upper = lax.broadcasted_iota(jnp.int32, (rows, rows), 0) <= lax.broadcasted_iota(jnp.int32, (rows, rows), 1)
    many = jnp.broadcast_to(chosen, (8, rows)).astype(bf16)
    rank = jnp.dot(many, upper.astype(bf16), preferred_element_type=f32)[0:1, :] - 1.0
    slot_ids = lax.broadcasted_iota(jnp.int32, (capacity, rows), 0).astype(f32)
    placing = jnp.where(rank == slot_ids, chosen, 0.0)
    placing_ref[...] = placing
    slots_ref[...] = jnp.dot(placing.astype(bf16), tokens[...], preferred_element_type=f32).astype(bf16)


def place(routes, tokens):
    rows, width = tokens.shape
    return pl.pallas_call(
        place_kernel,
        name="place_tokens",
        out_shape=[jax.ShapeDtypeStruct((rows // 4, rows), f32), jax.ShapeDtypeStruct((rows // 4, width), bf16)],
        in_specs=[VMEM] * 2,
        out_specs=[VMEM] * 2,
        compiler_params=pltpu.CompilerParams(vmem_limit_bytes=8 << 20),
        cost_estimate=pl.CostEstimate(flops=2 * 32 * rows * width, bytes_accessed=3 * rows * width, transcendentals=0),
    )(routes, tokens)


def local(tokens, routes, language, teacher, router_weight, gate_weight, up_weight, down_weight):
    tok_rows, width = tokens.shape
    capacity = tok_rows // 4
    experts = router_weight.shape[1]
    all_tokens = tok_rows * 64
    placing, token_slots = place(routes.T, tokens)

    own_gate, own_up = load(after(gate_weight, token_slots), up_weight)
    gates = [own_gate, twin(after(gate_weight, token_slots))]
    ups = [own_up, twin(after(up_weight, token_slots))]
    token_blocks = gather(token_slots, own_gate, gates[1], ups[1])
    downs = [down_weight, twin(after(down_weight, *token_blocks[1:]))]
    hidden, pre_gate, pre_up = hidden_units(token_blocks, gates, ups)
    terms = slot_terms(hidden, downs)

    tokens, teacher, routes, language = lax.optimization_barrier((tokens, teacher, routes, language, hidden))[:4]
    first_id = routes[:, 0]
    second_id = routes[:, 1]
    chosen = jnp.logical_or(first_id == 0, second_id == 0)
    other_id = jnp.where(first_id == 0, second_id, first_id).astype(f32)
    placing_half = placing.astype(bf16)
    teacher_slots = jnp.dot(placing_half, teacher, preferred_element_type=f32).astype(bf16)
    logits = jnp.dot(token_slots, router_weight, preferred_element_type=f32)
    other_slots = jnp.sum(placing * other_id[None, :], axis=1)
    filled = jnp.sum(placing, axis=1)
    columns = lax.broadcasted_iota(jnp.int32, logits.shape, 1).astype(f32)
    other_hot = (columns == other_slots[:, None]).astype(f32)
    squash = jax.nn.sigmoid(logits[:, 0] - jnp.sum(logits * other_hot, axis=1))
    gate_value = filled * squash
    gate_slope = filled * squash * (1.0 - squash)
    aux_lane = lax.broadcasted_iota(jnp.int32, (capacity, LANES), 1)
    aux = jnp.where(aux_lane == 0, gate_value[:, None], jnp.where(aux_lane == 1, gate_slope[:, None], other_slots[:, None]))
    plain = tokens.astype(f32) - teacher.astype(f32)
    plain_grad = plain.astype(bf16)
    plain_loss = jnp.where(chosen, 0.0, 0.5 * jnp.mean(plain * plain, axis=1))
    lang_hot = (language[:, None] + SHIFT == lax.broadcasted_iota(jnp.int32, (tok_rows, LANES), 1)).astype(f32)
    slot_langs = jnp.dot(placing_half, lang_hot.astype(bf16), preferred_element_type=f32)
    sub = lax.broadcasted_iota(jnp.int32, (8, LANES), 0)
    base = jnp.where(sub == 0, jnp.sum(plain_loss[:, None] * lang_hot, axis=0)[None, :], jnp.sum(lang_hot, axis=0)[None, :])

    combined, grad_slots, so_far = slots(scatter(terms), token_slots, teacher_slots, aux, slot_langs, base, router_weight.T)
    placed = lax.dot_general(placing_half, combined, TN, preferred_element_type=f32)
    layer_out = jnp.where(chosen[:, None], placed.astype(bf16), tokens)
    grad_blocks = gather(grad_slots, layer_out)

    summed = router_sum(token_blocks[:PLANE], grad_blocks[:PLANE], experts)
    summed = summed + twin(summed)
    gate_grad, up_grad = hidden_grads(grad_blocks, downs, after(pre_gate, summed), pre_up)
    summed = summed + lax.ppermute(summed, "expert", [(i, i ^ 1) for i in range(4)])
    back_terms = slot_grads(after(gate_grad, summed), up_grad, gates, ups)
    summed = summed + lax.ppermute(summed, "expert", [(i, i ^ 2) for i in range(4)])
    summed = summed + pair(summed)
    grad_router = summed[:, :width].T / all_tokens
    lang_loss = (summed[0, width:] / jnp.maximum(summed[1, width:], 1.0))[SHIFT : SHIFT + LANGS]

    own_back = sum(t.astype(f32) for t in scatter(list(back_terms)))
    slot_grad = (so_far + own_back).astype(bf16)
    placed_grad = lax.dot_general(placing_half, slot_grad, TN, preferred_element_type=f32)
    grad_tokens = jnp.where(chosen[:, None], placed_grad.astype(bf16), plain_grad)
    return (layer_out, grad_tokens, grad_router, lang_loss)


def solution(mesh):
    wide = Mesh(mesh.devices.reshape(4, 4, 2, 2, 4), ("expert", "x", "z", "core", "dp"))
    rows = ("dp", "expert", "x", "z", "core")
    hidden = ("x", "z", "core")
    return jax.shard_map(
        local,
        mesh=wide,
        in_specs=(
            P(rows, None),
            P(rows, None),
            P(rows),
            P(rows, None),
            P(),
            P(None, hidden),
            P(None, hidden),
            P(hidden, None),
        ),
        out_specs=(P(rows, None), P(rows, None), P("dp", None), P("dp")),
        check_vma=False,
    )
```

```python
import functools

import jax
import jax.numpy as jnp
from jax import lax
from jax.experimental import pallas as pl
from jax.experimental.pallas import tpu as pltpu
from jax.sharding import Mesh
from jax.sharding import PartitionSpec as P

LANGS = 101
LANES = 128
TILE = 256
BLOCKS = 8
PLANE = 4
NT = (((1,), (1,)), ((), ()))
TN = (((0,), (0,)), ((), ()))
f32 = jnp.float32
bf16 = jnp.bfloat16
GROUP = ("x", "z", "core", "dp")


def move(value, target):
    pairs = []
    for x in range(4):
        for z in range(8):
            for c in range(2):
                tx, tz, tc = target(x, z, c)
                spots = [((px % 4 * 2 + pz % 2) * 2 + pc) * 4 + pz % 8 // 2 for px, pz, pc in ((x, z, c), (tx, tz, tc))]
                pairs.append(tuple(spots))
    return lax.ppermute(value, GROUP, pairs)


def facing(z, c):
    return z + 1 - 2 * ((z + c) % 2)


def ahead(value):
    return move(value, lambda x, z, c: (x + 1 - 2 * c, z, c))


def behind(value):
    return move(value, lambda x, z, c: (x - 1 + 2 * c, z, c))


def across(value):
    return move(value, lambda x, z, c: (x, facing(z, c), c))


def ahead_across(value):
    return move(value, lambda x, z, c: (x + 1 - 2 * c, facing(z, c), c))


def behind_across(value):
    return move(value, lambda x, z, c: (x - 1 + 2 * c, facing(z, c), c))


def twin(value):
    return move(value, lambda x, z, c: (x, z, 1 - c))


def pair(value):
    return move(value, lambda x, z, c: (x, z + 1 - 2 * (z % 2), c))


def after(value, *others):
    return lax.optimization_barrier((value, *others))[0]


def gather(own, early, *late):
    f1 = ahead(own)
    b1 = behind(own)
    z0 = across(own)
    f1_late, b1_late = after(f1, early, *late), after(b1, early)
    x2 = ahead(f1_late)
    zf1 = across(f1_late)
    zb1 = across(b1_late)
    zx2 = behind_across(b1_late)
    return [own, f1, b1, x2, z0, zf1, zb1, zx2]


def add(*parts):
    return sum(p.astype(f32) for p in parts).astype(bf16)


def scatter(terms):
    own, f1, b1, x2, z0, zf1, zb1, zx2 = terms
    got_zx2 = ahead_across(zx2)
    got_x2 = behind(x2)
    got_zf1 = across(zf1)
    got_zb1 = across(zb1)
    got_z0 = across(after(z0, got_x2))
    got_f1 = behind(add(f1, got_x2, got_zf1))
    got_b1 = ahead(add(b1, got_zb1, got_zx2))
    return [own, got_z0, got_f1, got_b1], got_x2


def stack_rows(blocks, rows):
    each, width = blocks[0].shape[0], rows.shape[1]
    for b, block in enumerate(blocks):
        rows[b * each : (b + 1) * each] = block[:, :width]


VMEM = pl.BlockSpec(memory_space=pltpu.VMEM)
HBM = pl.BlockSpec(memory_space=pltpu.HBM)


def hidden_kernel(*refs):
    blocks, gates, ups = refs[:BLOCKS], refs[BLOCKS : BLOCKS + 2], refs[BLOCKS + 2 : BLOCKS + 4]
    hidden, pre_gate, pre_up, rows = refs[BLOCKS + 4 :]
    half = gates[0].shape[1]
    stack_rows(blocks, rows)
    for t in range(2 * half // TILE):
        which, col = t * TILE // half, t * TILE % half
        gate = jnp.dot(rows[...], gates[which][:, col : col + TILE], preferred_element_type=f32)
        up = jnp.dot(rows[...], ups[which][:, col : col + TILE], preferred_element_type=f32)
        pre_gate[:, t * TILE : (t + 1) * TILE] = gate
        pre_up[:, t * TILE : (t + 1) * TILE] = up
        hidden[:, t * TILE : (t + 1) * TILE] = (gate * jax.nn.sigmoid(gate) * up).astype(bf16)


def hidden_units(blocks, gates, ups):
    width, half = gates[0].shape
    rows = BLOCKS * blocks[0].shape[0]
    return pl.pallas_call(
        hidden_kernel,
        name="hidden_units",
        out_shape=[jax.ShapeDtypeStruct((rows, 2 * half), kind) for kind in (bf16, f32, f32)],
        in_specs=[VMEM] * (BLOCKS + 4),
        out_specs=[VMEM] * 3,
        scratch_shapes=[pltpu.VMEM((rows, width), bf16)],
        compiler_params=pltpu.CompilerParams(vmem_limit_bytes=20 << 20),
        cost_estimate=pl.CostEstimate(flops=8 * rows * width * half, bytes_accessed=8 * width * half, transcendentals=2 * rows * half),
    )(*blocks, *gates, *ups)


def slot_term_kernel(*refs):
    hidden, downs, outs = refs[0], refs[1:3], refs[3:]
    each, width = outs[0].shape
    half = downs[0].shape[0]
    for n in range(width // TILE):
        cols = pl.ds(n * TILE, TILE)
        total = jnp.dot(hidden[:, :half], downs[0][:, cols], preferred_element_type=f32)
        total = total + jnp.dot(hidden[:, half:], downs[1][:, cols], preferred_element_type=f32)
        part = total.astype(bf16)
        for b in range(BLOCKS):
            outs[b][:, cols] = part[b * each : (b + 1) * each]


def slot_terms(hidden, downs):
    rows = hidden.shape[0]
    half, width = downs[0].shape
    return pl.pallas_call(
        slot_term_kernel,
        name="slot_terms",
        out_shape=[jax.ShapeDtypeStruct((rows // BLOCKS, width), bf16)] * BLOCKS,
        in_specs=[VMEM] * 3,
        out_specs=[VMEM] * BLOCKS,
        compiler_params=pltpu.CompilerParams(vmem_limit_bytes=20 << 20),
        cost_estimate=pl.CostEstimate(flops=4 * rows * width * half, bytes_accessed=4 * width * half, transcendentals=0),
    )(hidden, *downs)


def hidden_grad_kernel(*refs):
    blocks, downs = refs[:BLOCKS], refs[BLOCKS : BLOCKS + 2]
    pre_gate, pre_up, gate_grad, up_grad, rows = refs[BLOCKS + 2 :]
    half = downs[0].shape[0]
    stack_rows(blocks, rows)
    for t in range(2 * half // TILE):
        which, row = t * TILE // half, t * TILE % half
        back = lax.dot_general(rows[...], downs[which][row : row + TILE, :], NT, preferred_element_type=f32)
        gate = pre_gate[:, t * TILE : (t + 1) * TILE]
        up = pre_up[:, t * TILE : (t + 1) * TILE]
        squash = jax.nn.sigmoid(gate)
        gate_grad[:, t * TILE : (t + 1) * TILE] = (back * up * squash * (1.0 + gate * (1.0 - squash))).astype(bf16)
        up_grad[:, t * TILE : (t + 1) * TILE] = (back * gate * squash).astype(bf16)


def hidden_grads(blocks, downs, pre_gate, pre_up):
    half, width = downs[0].shape
    rows = pre_gate.shape[0]
    return pl.pallas_call(
        hidden_grad_kernel,
        name="hidden_grads",
        out_shape=[jax.ShapeDtypeStruct((rows, 2 * half), bf16)] * 2,
        in_specs=[VMEM] * (BLOCKS + 4),
        out_specs=[VMEM] * 2,
        scratch_shapes=[pltpu.VMEM((rows, width), bf16)],
        compiler_params=pltpu.CompilerParams(vmem_limit_bytes=20 << 20),
        cost_estimate=pl.CostEstimate(flops=4 * rows * width * half, bytes_accessed=4 * width * half, transcendentals=2 * rows * half),
    )(*blocks, *downs, pre_gate, pre_up)


def slot_grad_kernel(*refs):
    gate_grad, up_grad = refs[:2]
    gates, ups, outs = refs[2:4], refs[4:6], refs[6:]
    each = outs[0].shape[0]
    width, half = gates[0].shape
    for n in range(width // TILE):
        cols = pl.ds(n * TILE, TILE)
        total = None
        for which in range(2):
            for grad, weights in ((gate_grad, gates), (up_grad, ups)):
                term = lax.dot_general(grad[:, which * half : (which + 1) * half], weights[which][cols, :], NT, preferred_element_type=f32)
                total = term if total is None else total + term
        part = total.astype(bf16)
        for b in range(BLOCKS):
            outs[b][:, cols] = part[b * each : (b + 1) * each]


def slot_grads(gate_grad, up_grad, gates, ups):
    width, half = gates[0].shape
    rows = gate_grad.shape[0]
    return pl.pallas_call(
        slot_grad_kernel,
        name="slot_grads",
        out_shape=[jax.ShapeDtypeStruct((rows // BLOCKS, width), bf16)] * BLOCKS,
        in_specs=[VMEM] * 6,
        out_specs=[VMEM] * BLOCKS,
        compiler_params=pltpu.CompilerParams(vmem_limit_bytes=20 << 20),
        cost_estimate=pl.CostEstimate(flops=8 * rows * width * half, bytes_accessed=8 * width * half, transcendentals=0),
    )(gate_grad, up_grad, *gates, *ups)


def three(value):
    high = value.astype(bf16).astype(f32)
    rest = value - high
    mid = rest.astype(bf16).astype(f32)
    return high, mid, rest - mid


SHIFT = 4


def slot_kernel(*refs):
    terms = refs[:4]
    tokens, teacher, aux, langs, base, router, combined_ref, grad_ref, so_far_ref = refs[4:]
    width = tokens.shape[1]
    aux = aux[...]
    gate_value, gate_slope, other = aux[:, 0:1], aux[:, 1:2], aux[:, 2:3]
    total = terms[0][...].astype(f32)
    for t in terms[1:]:
        total = total + t[...].astype(f32)
    combined = tokens[...].astype(f32) + gate_value * total
    combined_ref[...] = combined.astype(bf16)
    deviation = combined - teacher[...].astype(f32)
    grad_ref[:, :width] = (gate_value * deviation).astype(bf16)
    loss = jnp.sum(deviation * deviation, axis=1, keepdims=True) * (0.5 / width)
    dot = jnp.sum(deviation * total, axis=1, keepdims=True) * gate_slope
    lang_sums = base[0:1, :] + jnp.sum(loss * langs[...], axis=0, keepdims=True)
    rows = lax.broadcasted_iota(jnp.int32, langs.shape, 0)
    lanes = lax.broadcasted_iota(jnp.int32, langs.shape, 1)
    extra = jnp.zeros(langs.shape, f32)
    for i, (d, s) in enumerate(zip(three(dot) + (other,), three(lang_sums) + (base[1:2, :],))):
        extra = jnp.where(lanes == i, d, extra)
        extra = jnp.where(jnp.logical_and(rows == i, lanes >= SHIFT), s, extra)
    grad_ref[:, width:] = extra.astype(bf16)
    back = deviation
    columns = lax.broadcasted_iota(jnp.int32, (tokens.shape[0], router.shape[0]), 1)
    direction = (columns == 0).astype(f32) - (columns.astype(f32) == other).astype(f32)
    for part in three(dot):
        back = back + jnp.dot((part * direction).astype(bf16), router[...], preferred_element_type=f32)
    so_far_ref[...] = back


def slots(terms, tokens, teacher, aux, langs, base, router):
    each, width = tokens.shape
    return pl.pallas_call(
        slot_kernel,
        name="slot_step",
        out_shape=[
            jax.ShapeDtypeStruct((each, width), bf16),
            jax.ShapeDtypeStruct((each, width + LANES), bf16),
            jax.ShapeDtypeStruct((each, width), f32),
        ],
        in_specs=[VMEM] * 10,
        out_specs=[VMEM] * 3,
        compiler_params=pltpu.CompilerParams(vmem_limit_bytes=8 << 20),
        cost_estimate=pl.CostEstimate(flops=30 * each * width, bytes_accessed=24 * each * width, transcendentals=0),
    )(*terms, tokens, teacher, aux, langs, base, router)


def router_kernel(*refs):
    token_blocks, grad_blocks = refs[:PLANE], refs[PLANE : 2 * PLANE]
    out, rows = refs[2 * PLANE :]
    experts = out.shape[0]
    width = rows.shape[1]
    stack_rows(token_blocks, rows)
    each = token_blocks[0].shape[0]
    lanes = lax.broadcasted_iota(jnp.int32, (each, LANES), 1)
    expert = lanes % experts
    slopes, langs = [], jnp.zeros((each, LANES), f32)
    for b in range(PLANE):
        extra = grad_blocks[b][:, width:].astype(f32)
        langs = langs + extra
        other = extra[:, 3:4]
        direction = (expert == 0).astype(f32) - (expert.astype(f32) == other).astype(f32)
        part = jnp.where(lanes < experts, extra[:, 0:1], jnp.where(lanes < 2 * experts, extra[:, 1:2], extra[:, 2:3]))
        slopes.append(jnp.where(lanes < 3 * experts, part * direction, 0.0).astype(bf16))
    sums = lax.dot_general(jnp.concatenate(slopes, 0), rows[...], TN, preferred_element_type=f32)
    out[:, :width] = sums[:experts] + sums[experts : 2 * experts] + sums[2 * experts : 3 * experts]
    sub = lax.broadcasted_iota(jnp.int32, (experts, LANES), 0)
    out[:, width:] = jnp.where(sub == 0, langs[0:1] + langs[1:2] + langs[2:3], jnp.where(sub == 1, langs[3:4], 0.0))


def router_sum(token_blocks, grad_blocks, experts):
    each, width = token_blocks[0].shape
    return pl.pallas_call(
        router_kernel,
        name="router_sum",
        out_shape=jax.ShapeDtypeStruct((experts, width + LANES), f32),
        in_specs=[VMEM] * (2 * PLANE),
        out_specs=VMEM,
        scratch_shapes=[pltpu.VMEM((PLANE * each, width), bf16)],
        compiler_params=pltpu.CompilerParams(vmem_limit_bytes=12 << 20),
        cost_estimate=pl.CostEstimate(flops=2 * 128 * 128 * 3072, bytes_accessed=4 * 128 * 3072, transcendentals=0),
    )(*token_blocks, *grad_blocks)


def load_kernel(gate, up, gate_ref, up_ref, sems):
    copies = [pltpu.make_async_copy(gate, gate_ref, sems.at[0]), pltpu.make_async_copy(up, up_ref, sems.at[1])]
    for copy in copies:
        copy.start()
    for copy in copies:
        copy.wait()


def load(gate, up):
    return pl.pallas_call(
        load_kernel,
        name="load_weights",
        out_shape=[jax.ShapeDtypeStruct(w.shape, w.dtype) for w in (gate, up)],
        in_specs=[HBM] * 2,
        out_specs=[VMEM] * 2,
        scratch_shapes=[pltpu.SemaphoreType.DMA((2,))],
        compiler_params=pltpu.CompilerParams(vmem_limit_bytes=8 << 20),
        cost_estimate=pl.CostEstimate(flops=0, bytes_accessed=4 * gate.size, transcendentals=0),
    )(gate, up)


def place_kernel(routes, tokens, placing_ref, slots_ref):
    rows = tokens.shape[0]
    capacity = slots_ref.shape[0]
    chosen = jnp.logical_or(routes[0:1, :] == 0, routes[1:2, :] == 0).astype(f32)
    upper = lax.broadcasted_iota(jnp.int32, (rows, rows), 0) <= lax.broadcasted_iota(jnp.int32, (rows, rows), 1)
    many = jnp.broadcast_to(chosen, (8, rows)).astype(bf16)
    rank = jnp.dot(many, upper.astype(bf16), preferred_element_type=f32)[0:1, :] - 1.0
    slot_ids = lax.broadcasted_iota(jnp.int32, (capacity, rows), 0).astype(f32)
    placing = jnp.where(rank == slot_ids, chosen, 0.0)
    placing_ref[...] = placing
    slots_ref[...] = jnp.dot(placing.astype(bf16), tokens[...], preferred_element_type=f32).astype(bf16)


def place(routes, tokens):
    rows, width = tokens.shape
    return pl.pallas_call(
        place_kernel,
        name="place_tokens",
        out_shape=[jax.ShapeDtypeStruct((rows // 4, rows), f32), jax.ShapeDtypeStruct((rows // 4, width), bf16)],
        in_specs=[VMEM] * 2,
        out_specs=[VMEM] * 2,
        compiler_params=pltpu.CompilerParams(vmem_limit_bytes=8 << 20),
        cost_estimate=pl.CostEstimate(flops=2 * 32 * rows * width, bytes_accessed=3 * rows * width, transcendentals=0),
    )(routes, tokens)


def local(tokens, routes, language, teacher, router_weight, gate_weight, up_weight, down_weight):
    tok_rows, width = tokens.shape
    capacity = tok_rows // 4
    experts = router_weight.shape[1]
    all_tokens = tok_rows * 64
    placing, token_slots = place(routes.T, tokens)

    own_gate, own_up = load(after(gate_weight, token_slots), up_weight)
    gates = [own_gate, twin(after(gate_weight, token_slots))]
    ups = [own_up, twin(after(up_weight, token_slots))]
    token_blocks = gather(token_slots, own_gate, gates[1], ups[1])
    downs = [down_weight, twin(after(down_weight, *token_blocks[1:]))]
    hidden, pre_gate, pre_up = hidden_units(token_blocks, gates, ups)
    terms = slot_terms(hidden, downs)

    tokens, teacher, routes, language = lax.optimization_barrier((tokens, teacher, routes, language, hidden))[:4]
    first_id = routes[:, 0]
    second_id = routes[:, 1]
    chosen = jnp.logical_or(first_id == 0, second_id == 0)
    other_id = jnp.where(first_id == 0, second_id, first_id).astype(f32)
    placing_half = placing.astype(bf16)
    teacher_slots = jnp.dot(placing_half, teacher, preferred_element_type=f32).astype(bf16)
    logits = jnp.dot(token_slots, router_weight, preferred_element_type=f32)
    other_slots = jnp.sum(placing * other_id[None, :], axis=1)
    filled = jnp.sum(placing, axis=1)
    columns = lax.broadcasted_iota(jnp.int32, logits.shape, 1).astype(f32)
    other_hot = (columns == other_slots[:, None]).astype(f32)
    squash = jax.nn.sigmoid(logits[:, 0] - jnp.sum(logits * other_hot, axis=1))
    gate_value = filled * squash
    gate_slope = filled * squash * (1.0 - squash)
    aux_lane = lax.broadcasted_iota(jnp.int32, (capacity, LANES), 1)
    aux = jnp.where(aux_lane == 0, gate_value[:, None], jnp.where(aux_lane == 1, gate_slope[:, None], other_slots[:, None]))
    plain = tokens.astype(f32) - teacher.astype(f32)
    plain_grad = plain.astype(bf16)
    plain_loss = jnp.where(chosen, 0.0, 0.5 * jnp.mean(plain * plain, axis=1))
    lang_hot = (language[:, None] + SHIFT == lax.broadcasted_iota(jnp.int32, (tok_rows, LANES), 1)).astype(f32)
    slot_langs = jnp.dot(placing_half, lang_hot.astype(bf16), preferred_element_type=f32)
    sub = lax.broadcasted_iota(jnp.int32, (8, LANES), 0)
    base = jnp.where(sub == 0, jnp.sum(plain_loss[:, None] * lang_hot, axis=0)[None, :], jnp.sum(lang_hot, axis=0)[None, :])

    combined, grad_slots, so_far = slots(scatter(terms)[0], token_slots, teacher_slots, aux, slot_langs, base, router_weight.T)
    placed = lax.dot_general(placing_half, combined, TN, preferred_element_type=f32)
    layer_out = jnp.where(chosen[:, None], placed.astype(bf16), tokens)
    grad_blocks = gather(grad_slots, layer_out)

    summed = router_sum(token_blocks[:PLANE], grad_blocks[:PLANE], experts)
    summed = summed + twin(summed)
    gate_grad, up_grad = hidden_grads(grad_blocks, downs, after(pre_gate, summed), pre_up)
    summed = summed + lax.ppermute(summed, "expert", [(i, i ^ 1) for i in range(4)])
    back_terms = slot_grads(after(gate_grad, summed), up_grad, gates, ups)
    back_parts, first_part = scatter(list(back_terms))
    summed = after(summed, first_part)
    summed = summed + lax.ppermute(summed, "expert", [(i, i ^ 2) for i in range(4)])
    summed = summed + pair(summed)
    grad_router = summed[:, :width].T / all_tokens
    lang_loss = (summed[0, width:] / jnp.maximum(summed[1, width:], 1.0))[SHIFT : SHIFT + LANGS]

    own_back = sum(t.astype(f32) for t in back_parts)
    slot_grad = (so_far + own_back).astype(bf16)
    placed_grad = lax.dot_general(placing_half, slot_grad, TN, preferred_element_type=f32)
    grad_tokens = jnp.where(chosen[:, None], placed_grad.astype(bf16), plain_grad)
    return (layer_out, grad_tokens, grad_router, lang_loss)


def solution(mesh):
    wide = Mesh(mesh.devices.reshape(4, 4, 2, 2, 4), ("expert", "x", "z", "core", "dp"))
    rows = ("dp", "expert", "x", "z", "core")
    hidden = ("x", "z", "core")
    return jax.shard_map(
        local,
        mesh=wide,
        in_specs=(
            P(rows, None),
            P(rows, None),
            P(rows),
            P(rows, None),
            P(),
            P(None, hidden),
            P(None, hidden),
            P(hidden, None),
        ),
        out_specs=(P(rows, None), P(rows, None), P("dp", None), P("dp")),
        check_vma=False,
    )
```
